128 devices in a mesh: gx: 8 (over z, core), gy: 16 (over y, x).
Axes of the slice: x: 4, y: 4, z: 4, core: 2. Of those that a mesh axis runs over, the one named last changes fastest.
Arguments:
- coeffs: bfloat16 [16, 128, 256, 128], P('gx', 'gy'), may hold values from -0.25 to 0.25
- permit: float32 [16, 128, 256], P('gx', 'gy'), may hold values from 0.25 to 4
- shift_diag: float32 [16, 128, 128], P('gx', 'gy'), may hold values from 0.5 to 4
- codes: int32 [16, 128, 6], P('gx', 'gy'), may hold values from 0 to 8
- counts: int32 [16, 128], P('gx', 'gy'), may hold values from 1 to 6
- weights: float32 [16, 128, 6], P('gx', 'gy'), may hold values from 0.5 to 1.5
- vectors: bfloat16 [16, 128, 128, 128], P('gx', 'gy'), may hold values from -6 to 6
Outputs:
- factor: bfloat16 [16, 128, 128, 128], P('gx', 'gy')
- applied: bfloat16 [16, 128, 128, 128], P('gx', 'gy')
The draws below stay inside these ranges and needn't reach their ends.
Inputs may be any that keep to these rules, and one draw needn't show every extreme that they name: codes name one of the 3 x 3 blocks around a block, as in the reference program.
All inputs are finite; a program needn't handle non-finite values.
Results may differ from the reference program's by a relative error of at most 0.0051.
Values may be sent and summed in bfloat16 or wider, within the bound.
No kernel may reach another device: no remote copies, remote signals or barrier semaphores. Data moves between devices by JAX's collectives and lax.ppermute only.
A program may use at most 64 MiB of HBM per device.

```python
import math
import jax
import jax.numpy as jnp
from jax import lax

B = 128
R = 256
NV = 128
PAT = 6
BX = 16
BY = 128


def draw_coeffs(key, part):
    key_cols = jax.random.fold_in(key, 11)
    key_rows = jax.random.fold_in(key, 23)
    column_noise = jax.random.normal(key_cols, (BX, BY, R, B + 1), jnp.float32)
    row_common = jax.random.normal(key_rows, (BX, BY, R, 1), jnp.float32)
    mixed = column_noise[:, :, :, 1:] + 0.9 * column_noise[:, :, :, :-1] + 1.5 * row_common
    values = mixed * jnp.float32(0.031)
    values = jnp.clip(values, -0.25, 0.25)
    return values.astype(jnp.bfloat16)


def touch_ends(values, key, low, largest):
    shape = values.shape
    place = [jax.random.randint(jax.random.fold_in(key, axis), (), 0, shape[axis]) for axis in range(len(shape))]
    values = values.at[tuple(place)].set(low)
    longest = shape.index(max(shape))
    place[longest] = (place[longest] + 1) % shape[longest]
    return values.at[tuple(place)].set(largest)


def steps_of(rng, dims, cuts, low, high):
    def one(dim, blocks):
        heights = jax.random.uniform(jax.random.fold_in(jax.random.fold_in(rng, 6), dim), (blocks,), jnp.float32, low / len(cuts), high / len(cuts))
        return jnp.repeat(jnp.exp(heights), dims[dim] // blocks).reshape((-1,) + (1,) * (len(dims) - dim - 1))

    gain = one(*cuts[0])
    for cut in cuts[1:]:
        gain = gain * one(*cut)
    return gain


def noise(own_key, shape, spread, reach, cuts=(), kind=jnp.bfloat16):
    drawn = jax.random.normal(own_key, shape, jnp.float32) * spread
    if len(cuts) > 0:
        drawn = steps_of(own_key, shape, cuts, -0.22, 0.18) * drawn
    return jnp.clip(drawn, min=-reach, max=reach).astype(kind)


def setup_inputs(seed: int = 0) -> dict:
    keys = jax.random.split(jax.random.key(seed), 8)
    coeffs = draw_coeffs(jax.random.fold_in(keys[7], 71), 0)
    permit = jnp.clip(jnp.exp(math.log(4.0) - 2.7725887 * jax.random.uniform(keys[1], (BX, BY, R), jnp.float32) ** steps_of(keys[1], (BX, BY, R), ((0, 8), (1, 16)), -0.2, 0.2)), 0.25, 4.0)
    shift_diag = jnp.clip(jnp.exp(math.log(4.0) - 2.0794415 * jax.random.uniform(keys[2], (BX, BY, B), jnp.float32) ** steps_of(keys[2], (BX, BY, B), ((0, 8), (1, 16)), -0.2, 0.2)), 0.5, 4.0)
    codes = touch_ends(jax.random.randint(keys[3], (BX, BY, PAT), 0, 9), jax.random.fold_in(keys[3], 1), 0, 8).astype(jnp.int32)
    counts = touch_ends(jax.random.randint(keys[4], (BX, BY), 1, PAT + 1), jax.random.fold_in(keys[4], 1), 1, PAT).astype(jnp.int32)
    weights = jnp.clip(0.5 + 1.0 * jax.random.uniform(keys[5], (BX, BY, PAT), jnp.float32) ** steps_of(keys[5], (BX, BY, PAT), ((0, 8), (1, 16)), -0.2, 0.2), 0.5, 1.5)
    vectors = noise(keys[6], (BX, BY, B, NV), 1.0, 6.0, ((0, 8), (1, 16)))
    return dict(coeffs=coeffs, permit=permit, shift_diag=shift_diag, codes=codes, counts=counts, weights=weights, vectors=vectors)


def reference(coeffs, permit, shift_diag, codes, counts, weights, vectors):
    padded = jnp.pad(coeffs, ((1, 1), (1, 1), (0, 0), (0, 0)))
    columns = jnp.arange(BY)

    def block_row(row_at):
        window = lax.dynamic_slice_in_dim(padded, row_at, 3, 0)
        permit_row = permit[row_at]
        code_row = codes[row_at]
        count_row = counts[row_at]
        gram = jnp.zeros((BY, B, B), jnp.float32)
        for slot_num in range(PAT):
            slot_code = code_row[:, slot_num]
            neighbour = window[slot_code // 3, columns + slot_code % 3]
            scaled = (permit_row[:, :, None] * neighbour.astype(jnp.float32)).astype(jnp.bfloat16)
            product = jnp.einsum('yrk,yrl->ykl', scaled.astype(jnp.float32), neighbour.astype(jnp.float32))
            gram = gram + jnp.where((slot_num < count_row)[:, None, None], product, jnp.float32(0.0))
        system = gram + shift_diag[row_at][:, :, None] * jnp.eye(B, dtype=jnp.float32)
        cholesky_factor = jnp.linalg.cholesky(system)
        identity = jnp.broadcast_to(jnp.eye(B, dtype=system.dtype), system.shape)
        inverse = lax.linalg.triangular_solve(cholesky_factor, identity, left_side=True, lower=True)
        factor_row = inverse.astype(jnp.bfloat16)
        images = jnp.einsum('ykl,ykv->ylv', factor_row.astype(jnp.float32), vectors[row_at].astype(jnp.float32))
        return (factor_row, images)
    factor, images = lax.map(block_row, jnp.arange(BX))
    active = jnp.arange(PAT)[None, None, :] < counts[:, :, None]
    gathered_sum = jnp.zeros((BX + 2, BY + 2, B, NV), jnp.float32)
    for offset in range(9):
        weight_sum = jnp.sum(jnp.where(active & (codes == offset), weights, jnp.float32(0.0)), axis=-1)
        gathered_sum = gathered_sum.at[offset // 3:offset // 3 + BX, offset % 3:offset % 3 + BY].add(weight_sum[:, :, None, None] * images)
    applied = gathered_sum[1:-1, 1:-1].astype(jnp.bfloat16)
    return (factor, applied)
```

```python
import jax
import jax.numpy as jnp
from jax import lax
from jax.experimental import pallas as pl
from jax.experimental.pallas import tpu as pltpu
from jax.sharding import PartitionSpec as P

PANEL = 8
GROUP = 4


def shift(value, by_x, by_y):
    nx, ny = lax.axis_size("gx"), lax.axis_size("gy")
    pairs = [
        (x * ny + y, (x + by_x) * ny + y + by_y)
        for x in range(nx)
        for y in range(ny)
        if 0 <= x + by_x < nx and 0 <= y + by_y < ny
    ]
    return lax.ppermute(value, ("gx", "gy"), pairs)


def lower_inverse(mat, xs, blocks, order):
    lane = lax.broadcasted_iota(jnp.int32, (PANEL, order), 1)
    sub = lax.broadcasted_iota(jnp.int32, (PANEL, order), 0)
    lane_full = lax.broadcasted_iota(jnp.int32, (order, order), 1)
    row_full = lax.broadcasted_iota(jnp.int32, (order, order), 0)

    def step(kb, carry):
        r0 = pl.multiple_of(kb * PANEL, PANEL)
        in_diag = (lane >= r0) & (lane < r0 + PANEL)
        unit = jnp.where(lane - r0 == sub, jnp.float32(1.0), jnp.float32(0.0))
        later = lane >= r0 + PANEL
        clear = (lane_full >= r0) & (lane_full < r0 + PANEL) & (row_full >= r0 + PANEL)
        for g in range(0, blocks, GROUP):
            ms = range(g, g + GROUP)
            rows = [mat[m, pl.ds(r0, PANEL), :] for m in ms]
            cols = []
            for r in rows:
                rolled = pltpu.roll(r, order - r0, axis=1)
                cols.append(
                    [jnp.broadcast_to(rolled[:, k : k + 1], (PANEL, order)) for k in range(PANEL)]
                )
            rows = [jnp.where(in_diag, unit, r) for r in rows]
            for k in range(PANEL):
                for n in range(GROUP):
                    c = cols[n]
                    inv = 1.0 / c[k][k : k + 1, :]
                    mult = jnp.where(sub > k, c[k] * inv, jnp.float32(0.0))
                    for j in range(k + 1, PANEL):
                        c[j] = c[j] - mult * c[j][k : k + 1, :]
                    rows[n] = rows[n] - mult * rows[n][k : k + 1, :]
            for n, m in enumerate(ms):
                diag = cols[n][0]
                for k in range(1, PANEL):
                    diag = jnp.where(sub == k, cols[n][k], diag)
                r = rows[n] * lax.rsqrt(diag)
                xs[m, pl.ds(r0, PANEL), :] = r
                hi = r.astype(jnp.bfloat16).astype(jnp.float32)
                rest = r - hi
                mid = rest.astype(jnp.bfloat16).astype(jnp.float32)
                low = rest - mid
                zero = jnp.float32(0.0)
                hi_l = jnp.where(later, hi, zero)
                mid_l = jnp.where(later, mid, zero)
                low_l = jnp.where(later, low, zero)
                right = jnp.concatenate([hi, mid, hi, low, hi, mid], axis=0).astype(jnp.bfloat16)
                left = jnp.concatenate([hi_l, hi_l, mid_l, hi_l, low_l, mid_l], axis=0)
                left = left.T.astype(jnp.bfloat16)
                update = jnp.dot(left, right, preferred_element_type=jnp.float32)
                mat[m] = jnp.where(clear, zero, mat[m]) - update
        return carry

    lax.fori_loop(0, order // PANEL, step, 0)


def blocks_kernel(
    codes, counts, weights, permit, diag, own, low, high, left, right, vectors,
    factor, center, to_low, to_high, to_left, to_right,
    turned, mat, xs, acc,
):
    bx, by = own.shape[0], own.shape[1]
    order = own.shape[3]
    wide = by + 2
    blocks = bx * by
    slots = codes.shape[1]
    for x in range(bx):
        for y in range(by):
            turned[(x + 1) * wide + y + 1] = own[x, y].T
    for y in range(by):
        turned[y + 1] = low[y].T
        turned[(bx + 1) * wide + y + 1] = high[y].T
    for x in range(bx + 2):
        turned[x * wide] = left[x].T
        turned[x * wide + by + 1] = right[x].T

    row_full = lax.broadcasted_iota(jnp.int32, (order, order), 0)
    lane_full = lax.broadcasted_iota(jnp.int32, (order, order), 1)

    def target(i, s):
        code = codes[i, s]
        return (i // by + code // 3) * wide + i % by + code % 3

    def gram(i, carry):
        total = jnp.zeros((order, order), jnp.float32)
        scale = permit[pl.ds(i, 1), :]
        for s in range(slots):
            block = turned[target(i, s)]
            on = jnp.where(s < counts[0, i], jnp.float32(1.0), jnp.float32(0.0))
            scaled = ((scale * on) * block.astype(jnp.float32)).astype(jnp.bfloat16)
            total = total + lax.dot_general(
                scaled, block, (((1,), (1,)), ((), ())), preferred_element_type=jnp.float32
            )
        total = (total + total.T) * jnp.float32(0.5)
        mat[i] = total + jnp.where(row_full == lane_full, diag[pl.ds(i, 1), :], jnp.float32(0.0))
        return carry

    lax.fori_loop(0, blocks, gram, 0)
    lower_inverse(mat, xs, blocks, order)
    acc[...] = jnp.zeros(acc.shape, acc.dtype)

    def apply(i, carry):
        f = jnp.where(lane_full <= row_full, xs[i], jnp.float32(0.0))
        factor[i] = f.astype(jnp.bfloat16)
        image = jnp.dot(f.T.astype(jnp.bfloat16), vectors[i], preferred_element_type=jnp.float32)

        def add(s, c):
            n = target(i, s)
            acc[n] = acc[n] + weights[i, s] * image
            return c

        return lax.fori_loop(0, counts[0, i], add, carry)

    lax.fori_loop(0, blocks, apply, 0)
    for x in range(bx):
        center[x] = acc[pl.ds((x + 1) * wide + 1, by)]
    to_low[...] = acc[pl.ds(1, by)].astype(jnp.bfloat16)
    to_high[...] = acc[pl.ds((bx + 1) * wide + 1, by)].astype(jnp.bfloat16)
    for x in range(bx + 2):
        to_left[x] = acc[x * wide].astype(jnp.bfloat16)
        to_right[x] = acc[x * wide + by + 1].astype(jnp.bfloat16)


def add_kernel(center, low, high, left, right, c00, c02, c20, c22, out):
    bx, by = center.shape[0], center.shape[1]
    f32 = jnp.float32
    for x in range(bx):
        for y in range(by):
            v = center[x, y]
            if x == 0:
                v = v + low[y].astype(f32)
            if x == bx - 1:
                v = v + high[y].astype(f32)
            if y == 0:
                v = v + left[x].astype(f32)
            if y == by - 1:
                v = v + right[x].astype(f32)
            if x == 0 and y == 0:
                v = v + c00[...].astype(f32)
            if x == 0 and y == by - 1:
                v = v + c02[...].astype(f32)
            if x == bx - 1 and y == 0:
                v = v + c20[...].astype(f32)
            if x == bx - 1 and y == by - 1:
                v = v + c22[...].astype(f32)
            out[x, y] = v.astype(out.dtype)


def local_blocks(codes, counts, weights, permit, diag, own, low, high, left, right, vectors):
    bx, by, coupling, order = own.shape
    width = vectors.shape[3]
    blocks = bx * by
    slots = codes.shape[2]
    padded = (bx + 2) * (by + 2)
    smem = pl.BlockSpec(memory_space=pltpu.SMEM)
    vmem = pl.BlockSpec(memory_space=pltpu.VMEM)
    bf16, f32 = jnp.bfloat16, jnp.float32
    return pl.pallas_call(
        blocks_kernel,
        out_shape=(
            jax.ShapeDtypeStruct((blocks, order, order), bf16),
            jax.ShapeDtypeStruct((bx, by, order, width), f32),
            jax.ShapeDtypeStruct((by, order, width), bf16),
            jax.ShapeDtypeStruct((by, order, width), bf16),
            jax.ShapeDtypeStruct((bx + 2, order, width), bf16),
            jax.ShapeDtypeStruct((bx + 2, order, width), bf16),
        ),
        in_specs=[smem] * 3 + [vmem] * 8,
        out_specs=(vmem,) * 6,
        scratch_shapes=[
            pltpu.VMEM((padded, order, coupling), bf16),
            pltpu.VMEM((blocks, order, order), f32),
            pltpu.VMEM((blocks, order, order), f32),
            pltpu.VMEM((padded, order, width), f32),
        ],
        compiler_params=pltpu.CompilerParams(vmem_limit_bytes=40 * 1024 * 1024),
        name="blocks",
    )(
        codes.reshape(blocks, slots), counts.reshape(1, blocks), weights.reshape(blocks, slots),
        permit.reshape(blocks, coupling), diag.reshape(blocks, order),
        own, low, high, left, right, vectors.reshape(blocks, order, width),
    )


def local(coeffs, permit, shift_diag, codes, counts, weights, vectors):
    bx, by, coupling, order = coeffs.shape
    low = shift(coeffs[bx - 1], 1, 0)
    high = shift(coeffs[0], -1, 0)
    left_send = jnp.concatenate([low[None, by - 1], coeffs[:, by - 1], high[None, by - 1]], axis=0)
    right_send = jnp.concatenate([low[None, 0], coeffs[:, 0], high[None, 0]], axis=0)
    left = shift(left_send, 0, 1)
    right = shift(right_send, 0, -1)
    factor, center, to_low, to_high, to_left, to_right = local_blocks(
        codes, counts, weights, permit, shift_diag, coeffs, low, high, left, right, vectors
    )
    from_low = shift(to_high, 1, 0)
    from_high = shift(to_low, -1, 0)
    from_left = shift(to_right[1 : bx + 1], 0, 1)
    from_right = shift(to_left[1 : bx + 1], 0, -1)
    c00 = shift(to_right[bx + 1], 1, 1)
    c02 = shift(to_left[bx + 1], 1, -1)
    c20 = shift(to_right[0], -1, 1)
    c22 = shift(to_left[0], -1, -1)
    vmem = pl.BlockSpec(memory_space=pltpu.VMEM)
    applied = pl.pallas_call(
        add_kernel,
        out_shape=jax.ShapeDtypeStruct(center.shape, jnp.bfloat16),
        in_specs=[vmem] * 9,
        out_specs=vmem,
        compiler_params=pltpu.CompilerParams(vmem_limit_bytes=16 * 1024 * 1024),
        name="collect",
    )(center, from_low, from_high, from_left, from_right, c00, c02, c20, c22)
    return factor.reshape(bx, by, order, order), applied


def solution(mesh):
    placed = (
        P("gx", "gy", None, None),
        P("gx", "gy", None),
        P("gx", "gy", None),
        P("gx", "gy", None),
        P("gx", "gy"),
        P("gx", "gy", None),
        P("gx", "gy", None, None),
    )
    return jax.shard_map(
        local,
        mesh=mesh,
        in_specs=placed,
        out_specs=(P("gx", "gy", None, None), P("gx", "gy", None, None)),
        check_vma=False,
    )
```

```python
import jax
import jax.numpy as jnp
from jax import lax
from jax.experimental import pallas as pl
from jax.experimental.pallas import tpu as pltpu
from jax.sharding import PartitionSpec as P

PANEL = 8
BF16, F32 = jnp.bfloat16, jnp.float32
VMEM = pl.BlockSpec(memory_space=pltpu.VMEM)
SMEM = pl.BlockSpec(memory_space=pltpu.SMEM)


def call(body, outs, ins, scratch, name, mib, flops):
    return pl.pallas_call(
        body,
        out_shape=outs,
        in_specs=ins,
        out_specs=jax.tree.map(lambda _: VMEM, outs),
        scratch_shapes=scratch,
        compiler_params=pltpu.CompilerParams(vmem_limit_bytes=mib * 1024 * 1024),
        cost_estimate=pl.CostEstimate(flops=flops, bytes_accessed=4 * 1024 * 1024, transcendentals=0),
        name=name,
    )


def shift(value, axis, by):
    length = lax.axis_size(axis)
    return lax.ppermute(value, axis, [(i, i + by) for i in range(length) if 0 <= i + by < length])


def iotas(order):
    return (
        lax.broadcasted_iota(jnp.int32, (order, order), 0),
        lax.broadcasted_iota(jnp.int32, (order, order), 1),
    )


def lower_inverse(mat, xs, blocks, order):
    lane = lax.broadcasted_iota(jnp.int32, (PANEL, order), 1)
    sub = lax.broadcasted_iota(jnp.int32, (PANEL, order), 0)

    def step(kb, carry):
        r0 = pl.multiple_of(kb * PANEL, PANEL)
        in_diag = (lane >= r0) & (lane < r0 + PANEL)
        unit = jnp.where(lane - r0 == sub, F32(1.0), F32(0.0))
        rows = [mat[m, pl.ds(r0, PANEL), :] for m in range(blocks)]
        picks = [jnp.full((PANEL, order), r0 + k, jnp.int32) for k in range(PANEL)]
        cols = [[jnp.take_along_axis(r, pick, axis=1) for pick in picks] for r in rows]
        rows = [jnp.where(in_diag, unit, r) for r in rows]
        for k in range(PANEL):
            for n in range(blocks):
                c = cols[n]
                inv = 1.0 / c[k][k : k + 1, :]
                mult = jnp.where(sub > k, c[k] * inv, F32(0.0))
                for j in range(k + 1, PANEL):
                    c[j] = c[j] - mult * c[j][k : k + 1, :]
                rows[n] = rows[n] - mult * rows[n][k : k + 1, :]
        for n in range(blocks):
            diag = cols[n][0]
            for k in range(1, PANEL):
                diag = jnp.where(sub == k, cols[n][k], diag)
            rows[n] = rows[n] * lax.rsqrt(diag)
        for m in range(blocks):
            r = rows[m]
            xs[m, pl.ds(r0, PANEL), :] = r
            hi = r.astype(BF16).astype(F32)
            rest = r - hi
            mid = rest.astype(BF16).astype(F32)
            low = rest - mid
            right = jnp.concatenate([hi, mid, hi, low, hi, mid], axis=0).astype(BF16)
            left = jnp.concatenate([hi, hi, mid, hi, low, mid], axis=0).astype(BF16)
            update = lax.dot_general(
                left, right, (((0,), (0,)), ((), ())), preferred_element_type=F32
            )
            for t in range(0, order, PANEL):
                mat[m, t : t + PANEL] = (
                    jnp.where(in_diag, F32(0.0), mat[m, t : t + PANEL]) - update[t : t + PANEL]
                )
        return carry

    lax.fori_loop(0, order // PANEL, step, 0)


def gram_of(x, y, codes, counts, permit, diag, block_at):
    row, lane = iotas(diag.shape[2])
    total = jnp.zeros(row.shape, F32)
    scale = permit[x, pl.ds(y, 1), :]
    for s in range(codes.shape[2]):
        code = codes[x, y, s]
        block = block_at(code // 3, code % 3)
        on = jnp.where(s < counts[x, y], F32(1.0), F32(0.0))
        scaled = ((scale * on) * block.astype(F32)).astype(BF16)
        total = total + lax.dot_general(
            scaled, block, (((1,), (1,)), ((), ())), preferred_element_type=F32
        )
    total = (total + total.T) * F32(0.5)
    return total + jnp.where(row == lane, diag[x, pl.ds(y, 1), :], F32(0.0))


def image_of(factor, vector):
    return lax.dot_general(factor, vector, (((0,), (0,)), ((), ())), preferred_element_type=F32)


def inner_gram(codes, counts, permit, diag, own, low, high, mats, edge_turned, turned):
    bx, by = own.shape[0], own.shape[1]
    inner = by - 2
    for y in range(by):
        turned[y] = low[y].T
        turned[(bx + 1) * by + y] = high[y].T
        for x in range(bx):
            turned[(x + 1) * by + y] = own[x, y].T
    for p in range(bx + 2):
        for n, y in enumerate((0, 1, by - 2, by - 1)):
            edge_turned[p * 4 + n] = turned[p * by + y]

    def some(x, g):
        for u in range(inner // 2):
            y = g * (inner // 2) + u + 1
            mats[x * inner + y - 1] = gram_of(
                x, y, codes, counts, permit, diag,
                lambda dx, dy: turned[(x + dx) * by + y + dy - 1],
            )

    def body(h, carry):
        some(h // 2, h % 2)
        return carry

    lax.fori_loop(0, 2 * bx, body, 0)


def edge_all(
    codes, counts, weights, permit, diag, edge_turned, left, right, vectors,
    factors, part, to_left, to_right, turned, mats, xs, acc,
):
    bx, by = vectors.shape[0], vectors.shape[1]
    order = mats.shape[1]
    for p in range(bx + 2):
        turned[p * 6] = left[p].T
        turned[p * 6 + 5] = right[p].T
        for n in range(4):
            turned[p * 6 + 1 + n] = edge_turned[p * 4 + n]
    edges = [(x, side) for x in range(bx) for side in range(2)]
    for m, (x, side) in enumerate(edges):
        mats[m] = gram_of(
            x, side * (by - 1), codes, counts, permit, diag,
            lambda dx, dy: turned[(x + dx) * 6 + side * 3 + dy],
        )
    lower_inverse(mats, xs, len(edges), order)
    acc[...] = jnp.zeros(acc.shape, acc.dtype)
    row, lane = iotas(order)
    images = []
    for m, (x, side) in enumerate(edges):
        f = jnp.where(lane <= row, xs[m], F32(0.0)).astype(BF16)
        factors[m] = f
        images.append(image_of(f, vectors[x, side * (by - 1)]))
    for m, (x, side) in enumerate(edges):
        y = side * (by - 1)

        def add(s, c):
            code = codes[x, y, s]
            n = (x + code // 3) * 6 + side * 3 + code % 3
            acc[n] = acc[n] + weights[x, y, s] * images[m]
            return c

        lax.fori_loop(0, counts[x, y], add, 0)
    for p in range(bx + 2):
        to_left[p] = acc[p * 6].astype(BF16)
        to_right[p] = acc[p * 6 + 5].astype(BF16)
        for n in range(4):
            part[p * 4 + n] = acc[p * 6 + 1 + n]


def inner_all(
    codes, counts, weights, mats_in, part, edge_factors, vectors,
    factor, center, halo, mats, xs, acc,
):
    bx, by = vectors.shape[0], vectors.shape[1]
    inner = by - 2
    order = mats.shape[1]
    mats[...] = mats_in[...]
    lower_inverse(mats, xs, bx * inner, order)
    zero = jnp.zeros(acc.shape[1:], F32)
    for p in range(bx + 2):
        for y in range(2, by - 2):
            acc[p * by + y] = zero
        for n, y in enumerate((0, 1, by - 2, by - 1)):
            acc[p * by + y] = part[p * 4 + n]
    for x in range(bx):
        factor[x, 0] = edge_factors[2 * x]
        factor[x, by - 1] = edge_factors[2 * x + 1]
    row, lane = iotas(order)

    def body(h, carry):
        x = h // (inner // 2)
        images = []
        for u in range(2):
            y = (h % (inner // 2)) * 2 + u + 1
            f = jnp.where(lane <= row, xs[x * inner + y - 1], F32(0.0)).astype(BF16)
            factor[x, y] = f
            images.append(image_of(f, vectors[x, y]))
        for u in range(2):
            y = (h % (inner // 2)) * 2 + u + 1

            def add(s, c):
                code = codes[x, y, s]
                n = (x + code // 3) * by + y + code % 3 - 1
                acc[n] = acc[n] + weights[x, y, s] * images[u]
                return c

            lax.fori_loop(0, counts[x, y], add, 0)
        return carry

    lax.fori_loop(0, bx * inner // 2, body, 0)
    for y in range(by):
        halo[0, y] = acc[y]
        halo[1, y] = acc[(bx + 1) * by + y]
        for x in range(bx):
            center[x, y] = acc[(x + 1) * by + y]


def close_halo(halo, from_left, from_right, to_low, to_high):
    by = halo.shape[1]
    last = from_left.shape[0] - 1
    for out, h, p in ((to_low, 0, 0), (to_high, 1, last)):
        for y in range(by):
            v = halo[h, y]
            if y == 0:
                v = v + from_left[p].astype(F32)
            if y == by - 1:
                v = v + from_right[p].astype(F32)
            out[y] = v.astype(BF16)


def collect(center, low, high, left, right, out):
    bx, by = center.shape[0], center.shape[1]
    for x in range(bx):
        for y in range(by):
            v = center[x, y]
            if x == 0:
                v = v + low[y].astype(F32)
            if x == bx - 1:
                v = v + high[y].astype(F32)
            if y == 0:
                v = v + left[x + 1].astype(F32)
            if y == by - 1:
                v = v + right[x + 1].astype(F32)
            out[x, y] = v.astype(out.dtype)


def local(coeffs, permit, diag, codes, counts, weights, vectors):
    bx, by, coupling, order = coeffs.shape
    width = vectors.shape[3]
    rows, inner = bx + 2, by - 2
    shape = jax.ShapeDtypeStruct
    low = shift(coeffs[bx - 1], "gx", 1)
    high = shift(coeffs[0], "gx", -1)
    left_send = jnp.concatenate([low[None, by - 1], coeffs[:, by - 1], high[None, by - 1]], axis=0)
    right_send = jnp.concatenate([low[None, 0], coeffs[:, 0], high[None, 0]], axis=0)
    left = shift(left_send, "gy", 1)
    right = shift(right_send, "gy", -1)
    mats, edge_turned = call(
        inner_gram,
        (shape((bx * inner, order, order), F32), shape((rows * 4, order, coupling), BF16)),
        [SMEM] * 2 + [VMEM] * 5,
        [pltpu.VMEM((rows * by, order, coupling), BF16)],
        "inner_gram", 16, 4 * 10**9,
    )(codes, counts, permit, diag, coeffs, low, high)
    edge_factors, part, to_left, to_right = call(
        edge_all,
        (
            shape((2 * bx, order, order), BF16),
            shape((rows * 4, order, width), F32),
            shape((rows, order, width), BF16),
            shape((rows, order, width), BF16),
        ),
        [SMEM] * 3 + [VMEM] * 6,
        [
            pltpu.VMEM((rows * 6, order, coupling), BF16),
            pltpu.VMEM((2 * bx, order, order), F32),
            pltpu.VMEM((2 * bx, order, order), F32),
            pltpu.VMEM((rows * 6, order, width), F32),
        ],
        "edge_all", 16, 8 * 10**9,
    )(codes, counts, weights, permit, diag, edge_turned, left, right, vectors)
    from_left = shift(to_right, "gy", 1)
    from_right = shift(to_left, "gy", -1)
    factor, center, halo = call(
        inner_all,
        (
            shape((bx, by, order, order), BF16),
            shape((bx, by, order, width), F32),
            shape((2, by, order, width), F32),
        ),
        [SMEM] * 3 + [VMEM] * 4,
        [
            pltpu.VMEM((bx * inner, order, order), F32),
            pltpu.VMEM((bx * inner, order, order), F32),
            pltpu.VMEM((rows * by, order, width), F32),
        ],
        "inner_all", 20, 12 * 10**9,
    )(codes, counts, weights, mats, part, edge_factors, vectors)
    to_low, to_high = call(
        close_halo,
        (shape((by, order, width), BF16), shape((by, order, width), BF16)),
        [VMEM] * 3, [], "close_halo", 8, 10**8,
    )(halo, from_left, from_right)
    from_low = shift(to_high, "gx", 1)
    from_high = shift(to_low, "gx", -1)
    applied = call(
        collect, shape(center.shape, BF16), [VMEM] * 5, [], "collect", 8, 10**8,
    )(center, from_low, from_high, from_left, from_right)
    return factor, applied


def solution(mesh):
    placed = (
        P("gx", "gy", None, None),
        P("gx", "gy", None),
        P("gx", "gy", None),
        P("gx", "gy", None),
        P("gx", "gy"),
        P("gx", "gy", None),
        P("gx", "gy", None, None),
    )
    return jax.shard_map(
        local,
        mesh=mesh,
        in_specs=placed,
        out_specs=(P("gx", "gy", None, None), P("gx", "gy", None, None)),
        check_vma=False,
    )
```

```python
import jax
import jax.numpy as jnp
from jax import lax
from jax.experimental import pallas as pl
from jax.experimental.pallas import tpu as pltpu
from jax.sharding import PartitionSpec as P

PANEL = 8
BF16, F32 = jnp.bfloat16, jnp.float32
VMEM = pl.BlockSpec(memory_space=pltpu.VMEM)
SMEM = pl.BlockSpec(memory_space=pltpu.SMEM)


def call(body, outs, ins, scratch, name, mib, flops):
    return pl.pallas_call(
        body,
        out_shape=outs,
        in_specs=ins,
        out_specs=jax.tree.map(lambda _: VMEM, outs),
        scratch_shapes=scratch,
        compiler_params=pltpu.CompilerParams(vmem_limit_bytes=mib * 1024 * 1024),
        cost_estimate=pl.CostEstimate(flops=flops, bytes_accessed=4 * 1024 * 1024, transcendentals=0),
        name=name,
    )


def swap(value, axis, first):
    pairs = []
    for i in range(first, lax.axis_size(axis) - 1, 2):
        pairs += [(i, i + 1), (i + 1, i)]
    return lax.ppermute(value, axis, pairs)


def parity(axis):
    return lax.rem(lax.axis_index(axis), 2)


def iotas(order):
    return (
        lax.broadcasted_iota(jnp.int32, (order, order), 0),
        lax.broadcasted_iota(jnp.int32, (order, order), 1),
    )


def lower_inverse(mat, xs, blocks, order):
    lane = lax.broadcasted_iota(jnp.int32, (PANEL, order), 1)
    sub = lax.broadcasted_iota(jnp.int32, (PANEL, order), 0)

    def step(kb, carry):
        r0 = pl.multiple_of(kb * PANEL, PANEL)
        in_diag = (lane >= r0) & (lane < r0 + PANEL)
        unit = jnp.where(lane - r0 == sub, F32(1.0), F32(0.0))
        rows = [mat[m, pl.ds(r0, PANEL), :] for m in range(blocks)]
        picks = [jnp.full((PANEL, order), r0 + k, jnp.int32) for k in range(PANEL)]
        cols = [[jnp.take_along_axis(r, pick, axis=1) for pick in picks] for r in rows]
        rows = [jnp.where(in_diag, unit, r) for r in rows]
        for k in range(PANEL):
            for n in range(blocks):
                c = cols[n]
                inv = 1.0 / c[k][k : k + 1, :]
                mult = jnp.where(sub > k, c[k] * inv, F32(0.0))
                for j in range(k + 1, PANEL):
                    c[j] = c[j] - mult * c[j][k : k + 1, :]
                rows[n] = rows[n] - mult * rows[n][k : k + 1, :]
        for n in range(blocks):
            diag = cols[n][0]
            for k in range(1, PANEL):
                diag = jnp.where(sub == k, cols[n][k], diag)
            rows[n] = rows[n] * lax.rsqrt(diag)
        for m in range(blocks):
            r = rows[m]
            xs[m, pl.ds(r0, PANEL), :] = r
            hi = r.astype(BF16).astype(F32)
            rest = r - hi
            mid = rest.astype(BF16).astype(F32)
            low = rest - mid
            right = jnp.concatenate([hi, mid, hi, low, hi, mid], axis=0).astype(BF16)
            left = jnp.concatenate([hi, hi, mid, hi, low, mid], axis=0).astype(BF16)
            update = lax.dot_general(
                left, right, (((0,), (0,)), ((), ())), preferred_element_type=F32
            )
            for t in range(0, order, PANEL):
                mat[m, t : t + PANEL] = (
                    jnp.where(in_diag, F32(0.0), mat[m, t : t + PANEL]) - update[t : t + PANEL]
                )
        return carry

    lax.fori_loop(0, order // PANEL, step, 0)


def gram_of(x, y, codes, counts, permit, diag, block_at):
    row, lane = iotas(diag.shape[2])
    total = jnp.zeros(row.shape, F32)
    scale = permit[x, pl.ds(y, 1), :]
    for s in range(codes.shape[2]):
        code = codes[x, y, s]
        block = block_at(code // 3, code % 3)
        on = jnp.where(s < counts[x, y], F32(1.0), F32(0.0))
        scaled = ((scale * on) * block.astype(F32)).astype(BF16)
        total = total + lax.dot_general(
            scaled, block, (((1,), (1,)), ((), ())), preferred_element_type=F32
        )
    total = (total + total.T) * F32(0.5)
    return total + jnp.where(row == lane, diag[x, pl.ds(y, 1), :], F32(0.0))


def image_of(factor, vector):
    return lax.dot_general(factor, vector, (((0,), (0,)), ((), ())), preferred_element_type=F32)


def inner_gram(codes, counts, permit, diag, own, odd, even, mats, edge_turned, turned):
    bx, by = own.shape[0], own.shape[1]
    inner = by - 2
    px = parity("gx")
    for y in range(by):
        turned[px * (bx + 1) * by + y] = odd[y].T
        turned[(1 - px) * (bx + 1) * by + y] = even[y].T
        for x in range(bx):
            turned[(x + 1) * by + y] = own[x, y].T
    for p in range(bx + 2):
        for n, y in enumerate((0, 1, by - 2, by - 1)):
            edge_turned[p * 4 + n] = turned[p * by + y]

    def some(x, g):
        for u in range(inner // 2):
            y = g * (inner // 2) + u + 1
            mats[x * inner + y - 1] = gram_of(
                x, y, codes, counts, permit, diag,
                lambda dx, dy: turned[(x + dx) * by + y + dy - 1],
            )

    def body(h, carry):
        some(h // 2, h % 2)
        return carry

    lax.fori_loop(0, 2 * bx, body, 0)


def edge_all(
    codes, counts, weights, permit, diag, edge_turned, odd, even, vectors,
    factors, part, to_odd, to_even, turned, mats, xs, acc,
):
    bx, by = vectors.shape[0], vectors.shape[1]
    order = mats.shape[1]
    px, py = parity("gx"), parity("gy")
    for p in range(bx + 2):
        row = px * (bx + 1) if p == 0 else (1 - px) * (bx + 1) if p == bx + 1 else p
        turned[row * 6 + 5 * py] = odd[p].T
        turned[row * 6 + 5 * (1 - py)] = even[p].T
        for n in range(4):
            turned[p * 6 + 1 + n] = edge_turned[p * 4 + n]
    edges = [(x, side) for x in range(bx) for side in range(2)]
    for m, (x, side) in enumerate(edges):
        mats[m] = gram_of(
            x, side * (by - 1), codes, counts, permit, diag,
            lambda dx, dy: turned[(x + dx) * 6 + side * 3 + dy],
        )
    lower_inverse(mats, xs, len(edges), order)
    acc[...] = jnp.zeros(acc.shape, acc.dtype)
    row, lane = iotas(order)
    images = []
    for m, (x, side) in enumerate(edges):
        f = jnp.where(lane <= row, xs[m], F32(0.0)).astype(BF16)
        factors[m] = f
        images.append(image_of(f, vectors[x, side * (by - 1)]))
    for m, (x, side) in enumerate(edges):
        y = side * (by - 1)

        def add(s, c):
            code = codes[x, y, s]
            n = (x + code // 3) * 6 + side * 3 + code % 3
            acc[n] = acc[n] + weights[x, y, s] * images[m]
            return c

        lax.fori_loop(0, counts[x, y], add, 0)
    for p in range(bx + 2):
        to_odd[p] = acc[p * 6 + 5 * py].astype(BF16)
        to_even[p] = acc[p * 6 + 5 * (1 - py)].astype(BF16)
        for n in range(4):
            part[p * 4 + n] = acc[p * 6 + 1 + n]


def inner_all(
    codes, counts, weights, mats_in, part, edge_factors, vectors,
    factor, center, halo, mats, xs, acc,
):
    bx, by = vectors.shape[0], vectors.shape[1]
    inner = by - 2
    order = mats.shape[1]
    mats[...] = mats_in[...]
    lower_inverse(mats, xs, bx * inner, order)
    zero = jnp.zeros(acc.shape[1:], F32)
    for p in range(bx + 2):
        for y in range(2, by - 2):
            acc[p * by + y] = zero
        for n, y in enumerate((0, 1, by - 2, by - 1)):
            acc[p * by + y] = part[p * 4 + n]
    for x in range(bx):
        factor[x, 0] = edge_factors[2 * x]
        factor[x, by - 1] = edge_factors[2 * x + 1]
    row, lane = iotas(order)

    def body(h, carry):
        x = h // (inner // 2)
        images = []
        for u in range(2):
            y = (h % (inner // 2)) * 2 + u + 1
            f = jnp.where(lane <= row, xs[x * inner + y - 1], F32(0.0)).astype(BF16)
            factor[x, y] = f
            images.append(image_of(f, vectors[x, y]))
        for u in range(2):
            y = (h % (inner // 2)) * 2 + u + 1

            def add(s, c):
                code = codes[x, y, s]
                n = (x + code // 3) * by + y + code % 3 - 1
                acc[n] = acc[n] + weights[x, y, s] * images[u]
                return c

            lax.fori_loop(0, counts[x, y], add, 0)
        return carry

    lax.fori_loop(0, bx * inner // 2, body, 0)
    for y in range(by):
        halo[0, y] = acc[y]
        halo[1, y] = acc[(bx + 1) * by + y]
        for x in range(bx):
            center[x, y] = acc[(x + 1) * by + y]


def close_halo(halo, odd, even, to_odd, to_even):
    by = halo.shape[1]
    last = odd.shape[0] - 1
    px, py = parity("gx"), parity("gy")
    for out, h in ((to_odd, px), (to_even, 1 - px)):
        for y in range(1, by - 1):
            out[y] = halo[h, y].astype(BF16)
        for terms, y in ((odd, (by - 1) * py), (even, (by - 1) * (1 - py))):
            out[y] = (halo[h, y] + terms[h * last].astype(F32)).astype(BF16)


def collect(center, odd_x, even_x, odd_y, even_y, out):
    bx, by = center.shape[0], center.shape[1]
    px, py = parity("gx"), parity("gy")
    for terms, x in ((odd_x, (bx - 1) * px), (even_x, (bx - 1) * (1 - px))):
        for y in range(1, by - 1):
            out[x, y] = (center[x, y] + terms[y].astype(F32)).astype(BF16)
        for more, y in ((odd_y, (by - 1) * py), (even_y, (by - 1) * (1 - py))):
            v = center[x, y] + terms[y].astype(F32) + more[x + 1].astype(F32)
            out[x, y] = v.astype(BF16)


def local(coeffs, permit, diag, codes, counts, weights, vectors):
    bx, by, coupling, order = coeffs.shape
    width = vectors.shape[3]
    rows, inner = bx + 2, by - 2
    shape = jax.ShapeDtypeStruct
    px, py = parity("gx"), parity("gy")
    pick = lax.dynamic_index_in_dim

    def column(y):
        return jnp.concatenate([pick(odd_x, y, 0), pick(coeffs, y, 1, False), pick(even_x, y, 0)])

    odd_x = swap(pick(coeffs, (bx - 1) * px, 0, False), "gx", 1)
    even_x = swap(pick(coeffs, (bx - 1) * (1 - px), 0, False), "gx", 0)
    odd_y = swap(column((by - 1) * py), "gy", 1)
    even_y = swap(column((by - 1) * (1 - py)), "gy", 0)
    mats, edge_turned = call(
        inner_gram,
        (shape((bx * inner, order, order), F32), shape((rows * 4, order, coupling), BF16)),
        [SMEM] * 2 + [VMEM] * 5,
        [pltpu.VMEM((rows * by, order, coupling), BF16)],
        "inner_gram", 16, 4 * 10**9,
    )(codes, counts, permit, diag, coeffs, odd_x, even_x)
    edge_factors, part, to_odd, to_even = call(
        edge_all,
        (
            shape((2 * bx, order, order), BF16),
            shape((rows * 4, order, width), F32),
            shape((rows, order, width), BF16),
            shape((rows, order, width), BF16),
        ),
        [SMEM] * 3 + [VMEM] * 6,
        [
            pltpu.VMEM((rows * 6, order, coupling), BF16),
            pltpu.VMEM((2 * bx, order, order), F32),
            pltpu.VMEM((2 * bx, order, order), F32),
            pltpu.VMEM((rows * 6, order, width), F32),
        ],
        "edge_all", 16, 8 * 10**9,
    )(codes, counts, weights, permit, diag, edge_turned, odd_y, even_y, vectors)
    from_odd_y = swap(to_odd, "gy", 1)
    from_even_y = swap(to_even, "gy", 0)
    factor, center, halo = call(
        inner_all,
        (
            shape((bx, by, order, order), BF16),
            shape((bx, by, order, width), F32),
            shape((2, by, order, width), F32),
        ),
        [SMEM] * 3 + [VMEM] * 4,
        [
            pltpu.VMEM((bx * inner, order, order), F32),
            pltpu.VMEM((bx * inner, order, order), F32),
            pltpu.VMEM((rows * by, order, width), F32),
        ],
        "inner_all", 20, 12 * 10**9,
    )(codes, counts, weights, mats, part, edge_factors, vectors)
    to_odd, to_even = call(
        close_halo,
        (shape((by, order, width), BF16), shape((by, order, width), BF16)),
        [VMEM] * 3, [], "close_halo", 8, 10**8,
    )(halo, from_odd_y, from_even_y)
    from_odd_x = swap(to_odd, "gx", 1)
    from_even_x = swap(to_even, "gx", 0)
    applied = call(
        collect, shape(center.shape, BF16), [VMEM] * 5, [], "collect", 8, 10**8,
    )(center, from_odd_x, from_even_x, from_odd_y, from_even_y)
    return factor, applied


def solution(mesh):
    placed = (
        P("gx", "gy", None, None),
        P("gx", "gy", None),
        P("gx", "gy", None),
        P("gx", "gy", None),
        P("gx", "gy"),
        P("gx", "gy", None),
        P("gx", "gy", None, None),
    )
    return jax.shard_map(
        local,
        mesh=mesh,
        in_specs=placed,
        out_specs=(P("gx", "gy", None, None), P("gx", "gy", None, None)),
        check_vma=False,
    )
```

```python
import jax
import jax.numpy as jnp
from jax import lax
from jax.experimental import pallas as pl
from jax.experimental.pallas import tpu as pltpu
from jax.sharding import PartitionSpec as P

PANEL = 8
EARLY = 4
BF16, F32 = jnp.bfloat16, jnp.float32
VMEM = pl.BlockSpec(memory_space=pltpu.VMEM)
SMEM = pl.BlockSpec(memory_space=pltpu.SMEM)


def call(body, outs, ins, scratch, name, mib, flops):
    return pl.pallas_call(
        body,
        out_shape=outs,
        in_specs=ins,
        out_specs=jax.tree.map(lambda _: VMEM, outs),
        scratch_shapes=scratch,
        compiler_params=pltpu.CompilerParams(vmem_limit_bytes=mib * 1024 * 1024),
        cost_estimate=pl.CostEstimate(flops=flops, bytes_accessed=4 * 1024 * 1024, transcendentals=0),
        name=name,
    )


def swap(value, axis, first):
    pairs = []
    for i in range(first, lax.axis_size(axis) - 1, 2):
        pairs += [(i, i + 1), (i + 1, i)]
    return lax.ppermute(value, axis, pairs)


def parity(axis):
    return lax.rem(lax.axis_index(axis), 2)


def iotas(order):
    return (
        lax.broadcasted_iota(jnp.int32, (order, order), 0),
        lax.broadcasted_iota(jnp.int32, (order, order), 1),
    )


def eliminate(cols, rows, sub):
    for k in range(PANEL):
        for n, c in enumerate(cols):
            inv = 1.0 / c[k][k : k + 1, :]
            mult = jnp.where(sub > k, c[k] * inv, F32(0.0))
            for j in range(k + 1, PANEL):
                c[j] = c[j] - mult * c[j][k : k + 1, :]
            rows[n] = rows[n] - mult * rows[n][k : k + 1, :]
    rescale(cols, rows, sub)


def rescale(cols, rows, sub):
    for n, c in enumerate(cols):
        diag = c[0]
        for k in range(1, PANEL):
            diag = jnp.where(sub == k, c[k], diag)
        rows[n] = rows[n] * lax.rsqrt(diag)


def subtract(mat, m, parts, in_diag, order):
    hi, mid, low = [], [], []
    for r in parts:
        h = r.astype(BF16).astype(F32)
        rest = r - h
        c = rest.astype(BF16).astype(F32)
        hi.append(h)
        mid.append(c)
        low.append(rest - c)
    right = jnp.concatenate(hi + mid + hi + low + hi + mid, axis=0).astype(BF16)
    left = jnp.concatenate(hi + hi + mid + hi + low + mid, axis=0).astype(BF16)
    update = lax.dot_general(left, right, (((0,), (0,)), ((), ())), preferred_element_type=F32)
    for t in range(0, order, PANEL):
        mat[m, t : t + PANEL] = (
            jnp.where(in_diag, F32(0.0), mat[m, t : t + PANEL]) - update[t : t + PANEL]
        )


def spread(row, picks):
    return [jnp.take_along_axis(row, pick, axis=1) for pick in picks]


def lower_inverse(mat, xs, blocks, order, first, last):
    lane = lax.broadcasted_iota(jnp.int32, (PANEL, order), 1)
    sub = lax.broadcasted_iota(jnp.int32, (PANEL, order), 0)

    def step(kb, carry):
        r0 = pl.multiple_of(kb * PANEL, PANEL)
        in_diag = (lane >= r0) & (lane < r0 + PANEL)
        unit = jnp.where(lane - r0 == sub, F32(1.0), F32(0.0))
        picks = [jnp.full((PANEL, order), r0 + k, jnp.int32) for k in range(PANEL)]
        rows = [mat[m, pl.ds(r0, PANEL), :] for m in range(blocks)]
        cols = [spread(r, picks) for r in rows]
        rows = [jnp.where(in_diag, unit, r) for r in rows]
        eliminate(cols, rows, sub)
        for m in range(blocks):
            xs[m, pl.ds(r0, PANEL), :] = rows[m]
            subtract(mat, m, [rows[m]], in_diag, order)
        return carry

    lax.fori_loop(first, last, step, 0)


def lower_inverse_wide(mat, xs, blocks, order):
    lane = lax.broadcasted_iota(jnp.int32, (PANEL, order), 1)
    sub = lax.broadcasted_iota(jnp.int32, (PANEL, order), 0)

    def step(kb, carry):
        r0 = pl.multiple_of(kb * 2 * PANEL, 2 * PANEL)
        r1 = pl.multiple_of(r0 + PANEL, PANEL)
        in_top = (lane >= r0) & (lane < r1)
        in_bot = (lane >= r1) & (lane < r1 + PANEL)
        unit_top = jnp.where(lane - r0 == sub, F32(1.0), F32(0.0))
        unit_bot = jnp.where(lane - r1 == sub, F32(1.0), F32(0.0))
        picks = [jnp.full((PANEL, order), r0 + k, jnp.int32) for k in range(2 * PANEL)]
        top = [mat[m, pl.ds(r0, PANEL), :] for m in range(blocks)]
        bot = [mat[m, pl.ds(r1, PANEL), :] for m in range(blocks)]
        ctop = [spread(r, picks[:PANEL]) for r in top]
        cbot = [spread(r, picks[:PANEL]) for r in bot]
        top = [jnp.where(in_top, unit_top, r) for r in top]
        bot = [jnp.where(in_top, F32(0.0), r) for r in bot]
        for k in range(PANEL):
            for n in range(blocks):
                c, b = ctop[n], cbot[n]
                inv = 1.0 / c[k][k : k + 1, :]
                m0 = jnp.where(sub > k, c[k] * inv, F32(0.0))
                m1 = b[k] * inv
                for j in range(k + 1, PANEL):
                    row = c[j][k : k + 1, :]
                    c[j] = c[j] - m0 * row
                    b[j] = b[j] - m1 * row
                row = top[n][k : k + 1, :]
                top[n] = top[n] - m0 * row
                bot[n] = bot[n] - m1 * row
        cols = [spread(r, picks[PANEL:]) for r in bot]
        bot = [jnp.where(in_bot, unit_bot, r) for r in bot]
        rescale(ctop, top, sub)
        eliminate(cols, bot, sub)
        for m in range(blocks):
            upper = jnp.where(in_bot, F32(0.0), top[m])
            xs[m, pl.ds(r0, PANEL), :] = upper
            xs[m, pl.ds(r1, PANEL), :] = bot[m]
            subtract(mat, m, [upper, bot[m]], in_top | in_bot, order)
        return carry

    lax.fori_loop(0, order // (2 * PANEL), step, 0)


def gram_of(x, y, codes, counts, permit, diag, block_at):
    row, lane = iotas(diag.shape[2])
    total = jnp.zeros(row.shape, F32)
    scale = permit[x, pl.ds(y, 1), :]
    for s in range(codes.shape[2]):
        code = codes[x, y, s]
        block = block_at(code // 3, code % 3)
        on = jnp.where(s < counts[x, y], F32(1.0), F32(0.0))
        scaled = ((scale * on) * block.astype(F32)).astype(BF16)
        total = total + lax.dot_general(
            scaled, block, (((1,), (1,)), ((), ())), preferred_element_type=F32
        )
    total = (total + total.T) * F32(0.5)
    return total + jnp.where(row == lane, diag[x, pl.ds(y, 1), :], F32(0.0))


def image_of(factor, vector):
    return lax.dot_general(factor, vector, (((0,), (0,)), ((), ())), preferred_element_type=F32)


def inner_gram(codes, counts, permit, diag, own, odd, even, mats, xs, edge_turned, turned):
    bx, by = own.shape[0], own.shape[1]
    inner = by - 2
    px = parity("gx")
    for y in range(by):
        turned[px * (bx + 1) * by + y] = odd[y].T
        turned[(1 - px) * (bx + 1) * by + y] = even[y].T
        for x in range(bx):
            turned[(x + 1) * by + y] = own[x, y].T
    for p in range(bx + 2):
        for n, y in enumerate((0, 1, by - 2, by - 1)):
            edge_turned[p * 4 + n] = turned[p * by + y]

    def some(x, g):
        for u in range(inner // 2):
            y = g * (inner // 2) + u + 1
            mats[x * inner + y - 1] = gram_of(
                x, y, codes, counts, permit, diag,
                lambda dx, dy: turned[(x + dx) * by + y + dy - 1],
            )

    def body(h, carry):
        some(h // 2, h % 2)
        return carry

    lax.fori_loop(0, 2 * bx, body, 0)
    lower_inverse(mats, xs, bx * inner, mats.shape[1], 0, EARLY)


def edge_all(
    codes, counts, weights, permit, diag, edge_turned, odd, even, vectors,
    factors, part, to_odd, to_even, turned, mats, xs, acc,
):
    bx, by = vectors.shape[0], vectors.shape[1]
    order = mats.shape[1]
    px, py = parity("gx"), parity("gy")
    for p in range(bx + 2):
        row = px * (bx + 1) if p == 0 else (1 - px) * (bx + 1) if p == bx + 1 else p
        turned[row * 6 + 5 * py] = odd[p].T
        turned[row * 6 + 5 * (1 - py)] = even[p].T
        for n in range(4):
            turned[p * 6 + 1 + n] = edge_turned[p * 4 + n]
    edges = [(x, side) for x in range(bx) for side in range(2)]
    for m, (x, side) in enumerate(edges):
        mats[m] = gram_of(
            x, side * (by - 1), codes, counts, permit, diag,
            lambda dx, dy: turned[(x + dx) * 6 + side * 3 + dy],
        )
    lower_inverse_wide(mats, xs, len(edges), order)
    acc[...] = jnp.zeros(acc.shape, acc.dtype)
    row, lane = iotas(order)
    images = []
    for m, (x, side) in enumerate(edges):
        f = jnp.where(lane <= row, xs[m], F32(0.0)).astype(BF16)
        factors[m] = f
        images.append(image_of(f, vectors[x, side * (by - 1)]))
    for m, (x, side) in enumerate(edges):
        y = side * (by - 1)

        def add(s, c):
            code = codes[x, y, s]
            n = (x + code // 3) * 6 + side * 3 + code % 3
            acc[n] = acc[n] + weights[x, y, s] * images[m]
            return c

        lax.fori_loop(0, counts[x, y], add, 0)
    for p in range(bx + 2):
        to_odd[p] = acc[p * 6 + 5 * py].astype(BF16)
        to_even[p] = acc[p * 6 + 5 * (1 - py)].astype(BF16)
        for n in range(4):
            part[p * 4 + n] = acc[p * 6 + 1 + n]


def inner_all(
    codes, counts, weights, mats_in, xs_in, part, edge_factors, vectors,
    factor, center, halo, mats, xs, acc,
):
    bx, by = vectors.shape[0], vectors.shape[1]
    inner = by - 2
    order = mats.shape[1]
    done = EARLY * PANEL
    mats[:, done:] = mats_in[:, done:]
    xs[:, :done] = xs_in[:, :done]
    lower_inverse(mats, xs, bx * inner, order, EARLY, order // PANEL)
    zero = jnp.zeros(acc.shape[1:], F32)
    for p in range(bx + 2):
        for y in range(2, by - 2):
            acc[p * by + y] = zero
        for n, y in enumerate((0, 1, by - 2, by - 1)):
            acc[p * by + y] = part[p * 4 + n]
    for x in range(bx):
        factor[x, 0] = edge_factors[2 * x]
        factor[x, by - 1] = edge_factors[2 * x + 1]
    row, lane = iotas(order)

    def body(h, carry):
        x = h // (inner // 2)
        images = []
        for u in range(2):
            y = (h % (inner // 2)) * 2 + u + 1
            f = jnp.where(lane <= row, xs[x * inner + y - 1], F32(0.0)).astype(BF16)
            factor[x, y] = f
            images.append(image_of(f, vectors[x, y]))
        for u in range(2):
            y = (h % (inner // 2)) * 2 + u + 1

            def add(s, c):
                code = codes[x, y, s]
                n = (x + code // 3) * by + y + code % 3 - 1
                acc[n] = acc[n] + weights[x, y, s] * images[u]
                return c

            lax.fori_loop(0, counts[x, y], add, 0)
        return carry

    lax.fori_loop(0, bx * inner // 2, body, 0)
    for y in range(by):
        halo[0, y] = acc[y]
        halo[1, y] = acc[(bx + 1) * by + y]
        for x in range(bx):
            center[x, y] = acc[(x + 1) * by + y]


def close_halo(halo, odd, even, to_odd, to_even):
    by = halo.shape[1]
    last = odd.shape[0] - 1
    px, py = parity("gx"), parity("gy")
    for out, h in ((to_odd, px), (to_even, 1 - px)):
        for y in range(1, by - 1):
            out[y] = halo[h, y].astype(BF16)
        for terms, y in ((odd, (by - 1) * py), (even, (by - 1) * (1 - py))):
            out[y] = (halo[h, y] + terms[h * last].astype(F32)).astype(BF16)


def collect(center, odd_x, even_x, odd_y, even_y, out):
    bx, by = center.shape[0], center.shape[1]
    px, py = parity("gx"), parity("gy")
    for terms, x in ((odd_x, (bx - 1) * px), (even_x, (bx - 1) * (1 - px))):
        for y in range(1, by - 1):
            out[x, y] = (center[x, y] + terms[y].astype(F32)).astype(BF16)
        for more, y in ((odd_y, (by - 1) * py), (even_y, (by - 1) * (1 - py))):
            v = center[x, y] + terms[y].astype(F32) + more[x + 1].astype(F32)
            out[x, y] = v.astype(BF16)


def local(coeffs, permit, diag, codes, counts, weights, vectors):
    bx, by, coupling, order = coeffs.shape
    width = vectors.shape[3]
    rows, inner = bx + 2, by - 2
    shape = jax.ShapeDtypeStruct
    px, py = parity("gx"), parity("gy")
    pick = lax.dynamic_index_in_dim

    def column(y):
        return jnp.concatenate([pick(odd_x, y, 0), pick(coeffs, y, 1, False), pick(even_x, y, 0)])

    odd_x = swap(pick(coeffs, (bx - 1) * px, 0, False), "gx", 1)
    even_x = swap(pick(coeffs, (bx - 1) * (1 - px), 0, False), "gx", 0)
    odd_y = swap(column((by - 1) * py), "gy", 1)
    even_y = swap(column((by - 1) * (1 - py)), "gy", 0)
    mats, xs, edge_turned = call(
        inner_gram,
        (
            shape((bx * inner, order, order), F32),
            shape((bx * inner, order, order), F32),
            shape((rows * 4, order, coupling), BF16),
        ),
        [SMEM] * 2 + [VMEM] * 5,
        [pltpu.VMEM((rows * by, order, coupling), BF16)],
        "inner_gram", 16, 4 * 10**9,
    )(codes, counts, permit, diag, coeffs, odd_x, even_x)
    edge_factors, part, to_odd, to_even = call(
        edge_all,
        (
            shape((2 * bx, order, order), BF16),
            shape((rows * 4, order, width), F32),
            shape((rows, order, width), BF16),
            shape((rows, order, width), BF16),
        ),
        [SMEM] * 3 + [VMEM] * 6,
        [
            pltpu.VMEM((rows * 6, order, coupling), BF16),
            pltpu.VMEM((2 * bx, order, order), F32),
            pltpu.VMEM((2 * bx, order, order), F32),
            pltpu.VMEM((rows * 6, order, width), F32),
        ],
        "edge_all", 16, 8 * 10**9,
    )(codes, counts, weights, permit, diag, edge_turned, odd_y, even_y, vectors)
    from_odd_y = swap(to_odd, "gy", 1)
    from_even_y = swap(to_even, "gy", 0)
    factor, center, halo = call(
        inner_all,
        (
            shape((bx, by, order, order), BF16),
            shape((bx, by, order, width), F32),
            shape((2, by, order, width), F32),
        ),
        [SMEM] * 3 + [VMEM] * 5,
        [
            pltpu.VMEM((bx * inner, order, order), F32),
            pltpu.VMEM((bx * inner, order, order), F32),
            pltpu.VMEM((rows * by, order, width), F32),
        ],
        "inner_all", 20, 12 * 10**9,
    )(codes, counts, weights, mats, xs, part, edge_factors, vectors)
    to_odd, to_even = call(
        close_halo,
        (shape((by, order, width), BF16), shape((by, order, width), BF16)),
        [VMEM] * 3, [], "close_halo", 8, 10**8,
    )(halo, from_odd_y, from_even_y)
    from_odd_x = swap(to_odd, "gx", 1)
    from_even_x = swap(to_even, "gx", 0)
    applied = call(
        collect, shape(center.shape, BF16), [VMEM] * 5, [], "collect", 8, 10**8,
    )(center, from_odd_x, from_even_x, from_odd_y, from_even_y)
    return factor, applied


def solution(mesh):
    placed = (
        P("gx", "gy", None, None),
        P("gx", "gy", None),
        P("gx", "gy", None),
        P("gx", "gy", None),
        P("gx", "gy"),
        P("gx", "gy", None),
        P("gx", "gy", None, None),
    )
    return jax.shard_map(
        local,
        mesh=mesh,
        in_specs=placed,
        out_specs=(P("gx", "gy", None, None), P("gx", "gy", None, None)),
        check_vma=False,
    )
```

```python
import jax
import jax.numpy as jnp
from jax import lax
from jax.experimental import pallas as pl
from jax.experimental.pallas import tpu as pltpu
from jax.sharding import PartitionSpec as P

PANEL = 8
EARLY = 4
BF16, F32 = jnp.bfloat16, jnp.float32
VMEM = pl.BlockSpec(memory_space=pltpu.VMEM)
SMEM = pl.BlockSpec(memory_space=pltpu.SMEM)


def call(body, outs, ins, scratch, name, mib, flops):
    return pl.pallas_call(
        body,
        out_shape=outs,
        in_specs=ins,
        out_specs=jax.tree.map(lambda _: VMEM, outs),
        scratch_shapes=scratch,
        compiler_params=pltpu.CompilerParams(vmem_limit_bytes=mib * 1024 * 1024),
        cost_estimate=pl.CostEstimate(flops=flops, bytes_accessed=4 * 1024 * 1024, transcendentals=0),
        name=name,
    )


def swap(value, axis, first):
    pairs = []
    for i in range(first, lax.axis_size(axis) - 1, 2):
        pairs += [(i, i + 1), (i + 1, i)]
    return lax.ppermute(value, axis, pairs)


def parity(axis):
    return lax.rem(lax.axis_index(axis), 2)


def iotas(order):
    return (
        lax.broadcasted_iota(jnp.int32, (order, order), 0),
        lax.broadcasted_iota(jnp.int32, (order, order), 1),
    )


def eliminate(cols, rows, sub):
    for k in range(PANEL):
        for n, c in enumerate(cols):
            inv = 1.0 / c[k][k : k + 1, :]
            mult = jnp.where(sub > k, c[k] * inv, F32(0.0))
            for j in range(k + 1, PANEL):
                c[j] = c[j] - mult * c[j][k : k + 1, :]
            rows[n] = rows[n] - mult * rows[n][k : k + 1, :]
    rescale(cols, rows, sub)


def rescale(cols, rows, sub):
    for n, c in enumerate(cols):
        diag = c[0]
        for k in range(1, PANEL):
            diag = jnp.where(sub == k, c[k], diag)
        rows[n] = rows[n] * lax.rsqrt(diag)


def subtract(mat, m, parts, in_diag, order):
    hi, mid, low = [], [], []
    for r in parts:
        h = r.astype(BF16).astype(F32)
        rest = r - h
        c = rest.astype(BF16).astype(F32)
        hi.append(h)
        mid.append(c)
        low.append(rest - c)
    right = jnp.concatenate(hi + mid + hi + low + hi + mid, axis=0).astype(BF16)
    left = jnp.concatenate(hi + hi + mid + hi + low + mid, axis=0).astype(BF16)
    update = lax.dot_general(left, right, (((0,), (0,)), ((), ())), preferred_element_type=F32)
    for t in range(0, order, PANEL):
        mat[m, t : t + PANEL] = (
            jnp.where(in_diag, F32(0.0), mat[m, t : t + PANEL]) - update[t : t + PANEL]
        )


def spread(row, picks):
    return [jnp.take_along_axis(row, pick, axis=1) for pick in picks]


def lower_inverse(mat, xs, blocks, order, first, last):
    lane = lax.broadcasted_iota(jnp.int32, (PANEL, order), 1)
    sub = lax.broadcasted_iota(jnp.int32, (PANEL, order), 0)

    def step(kb, carry):
        r0 = pl.multiple_of(kb * PANEL, PANEL)
        in_diag = (lane >= r0) & (lane < r0 + PANEL)
        unit = jnp.where(lane - r0 == sub, F32(1.0), F32(0.0))
        picks = [jnp.full((PANEL, order), r0 + k, jnp.int32) for k in range(PANEL)]
        rows = [mat[m, pl.ds(r0, PANEL), :] for m in range(blocks)]
        cols = [spread(r, picks) for r in rows]
        rows = [jnp.where(in_diag, unit, r) for r in rows]
        eliminate(cols, rows, sub)
        for m in range(blocks):
            xs[m, pl.ds(r0, PANEL), :] = rows[m]
            subtract(mat, m, [rows[m]], in_diag, order)
        return carry

    lax.fori_loop(first, last, step, 0)


def lower_inverse_wide(mat, xs, blocks, order):
    lane = lax.broadcasted_iota(jnp.int32, (PANEL, order), 1)
    sub = lax.broadcasted_iota(jnp.int32, (PANEL, order), 0)

    def step(kb, carry):
        r0 = pl.multiple_of(kb * 2 * PANEL, 2 * PANEL)
        r1 = pl.multiple_of(r0 + PANEL, PANEL)
        in_top = (lane >= r0) & (lane < r1)
        in_bot = (lane >= r1) & (lane < r1 + PANEL)
        unit_top = jnp.where(lane - r0 == sub, F32(1.0), F32(0.0))
        unit_bot = jnp.where(lane - r1 == sub, F32(1.0), F32(0.0))
        picks = [jnp.full((PANEL, order), r0 + k, jnp.int32) for k in range(2 * PANEL)]
        top = [mat[m, pl.ds(r0, PANEL), :] for m in range(blocks)]
        bot = [mat[m, pl.ds(r1, PANEL), :] for m in range(blocks)]
        ctop = [spread(r, picks[:PANEL]) for r in top]
        cbot = [spread(r, picks[:PANEL]) for r in bot]
        top = [jnp.where(in_top, unit_top, r) for r in top]
        bot = [jnp.where(in_top, F32(0.0), r) for r in bot]
        for k in range(PANEL):
            for n in range(blocks):
                c, b = ctop[n], cbot[n]
                inv = 1.0 / c[k][k : k + 1, :]
                m0 = jnp.where(sub > k, c[k] * inv, F32(0.0))
                m1 = b[k] * inv
                for j in range(k + 1, PANEL):
                    row = c[j][k : k + 1, :]
                    c[j] = c[j] - m0 * row
                    b[j] = b[j] - m1 * row
                row = top[n][k : k + 1, :]
                top[n] = top[n] - m0 * row
                bot[n] = bot[n] - m1 * row
        cols = [spread(r, picks[PANEL:]) for r in bot]
        bot = [jnp.where(in_bot, unit_bot, r) for r in bot]
        rescale(ctop, top, sub)
        eliminate(cols, bot, sub)
        for m in range(blocks):
            upper = jnp.where(in_bot, F32(0.0), top[m])
            xs[m, pl.ds(r0, PANEL), :] = upper
            xs[m, pl.ds(r1, PANEL), :] = bot[m]
            subtract(mat, m, [upper, bot[m]], in_top | in_bot, order)
        return carry

    lax.fori_loop(0, order // (2 * PANEL), step, 0)


def gram_of(x, y, codes, counts, permit, diag, block_at):
    row, lane = iotas(diag.shape[2])
    total = jnp.zeros(row.shape, F32)
    scale = permit[x, pl.ds(y, 1), :]
    for s in range(codes.shape[2]):
        code = codes[x, y, s]
        block = block_at(code // 3, code % 3)
        on = jnp.where(s < counts[x, y], F32(1.0), F32(0.0))
        scaled = ((scale * on) * block.astype(F32)).astype(BF16)
        total = total + lax.dot_general(
            scaled, block, (((1,), (1,)), ((), ())), preferred_element_type=F32
        )
    total = (total + total.T) * F32(0.5)
    return total + jnp.where(row == lane, diag[x, pl.ds(y, 1), :], F32(0.0))


def image_of(factor, vector):
    return lax.dot_general(factor, vector, (((0,), (0,)), ((), ())), preferred_element_type=F32)


def inner_gram(codes, counts, permit, diag, own, odd, even, mats, xs, turned):
    bx, by = own.shape[0], own.shape[1]
    inner = by - 2
    px = parity("gx")
    for y in range(by):
        turned[px * (bx + 1) * by + y] = odd[y].T
        turned[(1 - px) * (bx + 1) * by + y] = even[y].T
        for x in range(bx):
            turned[(x + 1) * by + y] = own[x, y].T

    def some(x, g):
        for u in range(inner // 2):
            y = g * (inner // 2) + u + 1
            mats[x * inner + y - 1] = gram_of(
                x, y, codes, counts, permit, diag,
                lambda dx, dy: turned[(x + dx) * by + y + dy - 1],
            )

    def body(h, carry):
        some(h // 2, h % 2)
        return carry

    lax.fori_loop(0, 2 * bx, body, 0)
    lower_inverse(mats, xs, bx * inner, mats.shape[1], 0, EARLY)


def edge_all(
    codes, counts, weights, permit, diag, inner_turned, odd, even, vectors,
    factors, acc, to_odd, to_even, turned, mats, xs,
):
    bx, by = vectors.shape[0], vectors.shape[1]
    order = mats.shape[1]
    px, py = parity("gx"), parity("gy")
    for p in range(bx + 2):
        row = px * (bx + 1) if p == 0 else (1 - px) * (bx + 1) if p == bx + 1 else p
        turned[row * 6 + 5 * py] = odd[p].T
        turned[row * 6 + 5 * (1 - py)] = even[p].T
        for n, y in enumerate((0, 1, by - 2, by - 1)):
            turned[p * 6 + 1 + n] = inner_turned[p * by + y]
    edges = [(x, side) for x in range(bx) for side in range(2)]
    for m, (x, side) in enumerate(edges):
        mats[m] = gram_of(
            x, side * (by - 1), codes, counts, permit, diag,
            lambda dx, dy: turned[(x + dx) * 6 + side * 3 + dy],
        )
    lower_inverse_wide(mats, xs, len(edges), order)
    acc[...] = jnp.zeros(acc.shape, acc.dtype)
    row, lane = iotas(order)
    images = []
    for m, (x, side) in enumerate(edges):
        f = jnp.where(lane <= row, xs[m], F32(0.0)).astype(BF16)
        factors[m] = f
        images.append(image_of(f, vectors[x, side * (by - 1)]))
    for m, (x, side) in enumerate(edges):
        y = side * (by - 1)

        def add(s, c):
            code = codes[x, y, s]
            n = (x + code // 3) * 6 + side * 3 + code % 3
            acc[n] = acc[n] + weights[x, y, s] * images[m]
            return c

        lax.fori_loop(0, counts[x, y], add, 0)
    for p in range(bx + 2):
        to_odd[p] = acc[p * 6 + 5 * py].astype(BF16)
        to_even[p] = acc[p * 6 + 5 * (1 - py)].astype(BF16)


def inner_all(
    codes, counts, weights, mats_in, xs_in, edge_acc, edge_factors, vectors,
    factor, acc, mats, xs,
):
    bx, by = vectors.shape[0], vectors.shape[1]
    inner = by - 2
    order = mats.shape[1]
    done = EARLY * PANEL
    mats[:, done:] = mats_in[:, done:]
    xs[:, :done] = xs_in[:, :done]
    lower_inverse(mats, xs, bx * inner, order, EARLY, order // PANEL)
    zero = jnp.zeros(acc.shape[1:], F32)
    for p in range(bx + 2):
        for y in range(2, by - 2):
            acc[p * by + y] = zero
        for n, y in enumerate((0, 1, by - 2, by - 1)):
            acc[p * by + y] = edge_acc[p * 6 + 1 + n]
    for x in range(bx):
        factor[x, 0] = edge_factors[2 * x]
        factor[x, by - 1] = edge_factors[2 * x + 1]
    row, lane = iotas(order)

    def body(h, carry):
        x = h // (inner // 2)
        images = []
        for u in range(2):
            y = (h % (inner // 2)) * 2 + u + 1
            f = jnp.where(lane <= row, xs[x * inner + y - 1], F32(0.0)).astype(BF16)
            factor[x, y] = f
            images.append(image_of(f, vectors[x, y]))
        for u in range(2):
            y = (h % (inner // 2)) * 2 + u + 1

            def add(s, c):
                code = codes[x, y, s]
                n = (x + code // 3) * by + y + code % 3 - 1
                acc[n] = acc[n] + weights[x, y, s] * images[u]
                return c

            lax.fori_loop(0, counts[x, y], add, 0)
        return carry

    lax.fori_loop(0, bx * inner // 2, body, 0)


def close_halo(acc, odd, even, to_odd, to_even):
    by = to_odd.shape[0]
    last = odd.shape[0] - 1
    px, py = parity("gx"), parity("gy")
    for out, h in ((to_odd, px), (to_even, 1 - px)):
        row = h * last * by
        for y in range(1, by - 1):
            out[y] = acc[row + y].astype(BF16)
        for terms, y in ((odd, (by - 1) * py), (even, (by - 1) * (1 - py))):
            out[y] = (acc[row + y] + terms[h * last].astype(F32)).astype(BF16)


def collect(acc, odd_x, even_x, odd_y, even_y, out):
    bx, by = out.shape[0], out.shape[1]
    px, py = parity("gx"), parity("gy")
    for terms, x in ((odd_x, (bx - 1) * px), (even_x, (bx - 1) * (1 - px))):
        row = (x + 1) * by
        for y in range(1, by - 1):
            out[x, y] = (acc[row + y] + terms[y].astype(F32)).astype(BF16)
        for more, y in ((odd_y, (by - 1) * py), (even_y, (by - 1) * (1 - py))):
            v = acc[row + y] + terms[y].astype(F32) + more[x + 1].astype(F32)
            out[x, y] = v.astype(BF16)


def local(coeffs, permit, diag, codes, counts, weights, vectors):
    bx, by, coupling, order = coeffs.shape
    width = vectors.shape[3]
    rows, inner = bx + 2, by - 2
    shape = jax.ShapeDtypeStruct
    px, py = parity("gx"), parity("gy")
    pick = lax.dynamic_index_in_dim

    def column(y):
        return jnp.concatenate([pick(odd_x, y, 0), pick(coeffs, y, 1, False), pick(even_x, y, 0)])

    again = lax.optimization_barrier(coeffs)
    even_x = swap(pick(again, (bx - 1) * (1 - px), 0, False), "gx", 0)
    odd_x = swap(pick(coeffs, (bx - 1) * px, 0, False), "gx", 1)
    odd_y = swap(column((by - 1) * py), "gy", 1)
    even_y = swap(column((by - 1) * (1 - py)), "gy", 0)
    mats, xs, turned = call(
        inner_gram,
        (
            shape((bx * inner, order, order), F32),
            shape((bx * inner, order, order), F32),
            shape((rows * by, order, coupling), BF16),
        ),
        [SMEM] * 2 + [VMEM] * 5,
        [],
        "inner_gram", 16, 4 * 10**9,
    )(codes, counts, permit, diag, coeffs, odd_x, even_x)
    edge_factors, edge_acc, to_odd, to_even = call(
        edge_all,
        (
            shape((2 * bx, order, order), BF16),
            shape((rows * 6, order, width), F32),
            shape((rows, order, width), BF16),
            shape((rows, order, width), BF16),
        ),
        [SMEM] * 3 + [VMEM] * 6,
        [
            pltpu.VMEM((rows * 6, order, coupling), BF16),
            pltpu.VMEM((2 * bx, order, order), F32),
            pltpu.VMEM((2 * bx, order, order), F32),
        ],
        "edge_all", 16, 8 * 10**9,
    )(codes, counts, weights, permit, diag, turned, odd_y, even_y, vectors)
    from_odd_y = swap(to_odd, "gy", 1)
    from_even_y = swap(to_even, "gy", 0)
    factor, acc = call(
        inner_all,
        (
            shape((bx, by, order, order), BF16),
            shape((rows * by, order, width), F32),
        ),
        [SMEM] * 3 + [VMEM] * 5,
        [
            pltpu.VMEM((bx * inner, order, order), F32),
            pltpu.VMEM((bx * inner, order, order), F32),
        ],
        "inner_all", 20, 12 * 10**9,
    )(codes, counts, weights, mats, xs, edge_acc, edge_factors, vectors)
    to_odd, to_even = call(
        close_halo,
        (shape((by, order, width), BF16), shape((by, order, width), BF16)),
        [VMEM] * 3, [], "close_halo", 8, 10**8,
    )(acc, from_odd_y, from_even_y)
    from_odd_x = swap(to_odd, "gx", 1)
    from_even_x = swap(to_even, "gx", 0)
    applied = call(
        collect, shape((bx, by, order, width), BF16), [VMEM] * 5, [], "collect", 8, 10**8,
    )(acc, from_odd_x, from_even_x, from_odd_y, from_even_y)
    return factor, applied


def solution(mesh):
    placed = (
        P("gx", "gy", None, None),
        P("gx", "gy", None),
        P("gx", "gy", None),
        P("gx", "gy", None),
        P("gx", "gy"),
        P("gx", "gy", None),
        P("gx", "gy", None, None),
    )
    return jax.shard_map(
        local,
        mesh=mesh,
        in_specs=placed,
        out_specs=(P("gx", "gy", None, None), P("gx", "gy", None, None)),
        check_vma=False,
    )
```

```python
import jax
import jax.numpy as jnp
from jax import lax
from jax.experimental import pallas as pl
from jax.experimental.pallas import tpu as pltpu
from jax.sharding import PartitionSpec as P

PANEL = 8
EARLY = 6
BF16, F32 = jnp.bfloat16, jnp.float32
VMEM = pl.BlockSpec(memory_space=pltpu.VMEM)
SMEM = pl.BlockSpec(memory_space=pltpu.SMEM)


def call(body, outs, ins, scratch, name, mib, flops):
    return pl.pallas_call(
        body,
        out_shape=outs,
        in_specs=ins,
        out_specs=jax.tree.map(lambda _: VMEM, outs),
        scratch_shapes=scratch,
        compiler_params=pltpu.CompilerParams(vmem_limit_bytes=mib * 1024 * 1024),
        cost_estimate=pl.CostEstimate(flops=flops, bytes_accessed=4 * 1024 * 1024, transcendentals=0),
        name=name,
    )


def swap(value, axis, first):
    pairs = []
    for i in range(first, lax.axis_size(axis) - 1, 2):
        pairs += [(i, i + 1), (i + 1, i)]
    return lax.ppermute(value, axis, pairs)


def parity(axis):
    return lax.rem(lax.axis_index(axis), 2)


def iotas(order):
    return (
        lax.broadcasted_iota(jnp.int32, (order, order), 0),
        lax.broadcasted_iota(jnp.int32, (order, order), 1),
    )


def eliminate(cols, rows, sub):
    for k in range(PANEL):
        for n, c in enumerate(cols):
            inv = 1.0 / c[k][k : k + 1, :]
            mult = jnp.where(sub > k, c[k] * inv, F32(0.0))
            for j in range(k + 1, PANEL):
                c[j] = c[j] - mult * c[j][k : k + 1, :]
            rows[n] = rows[n] - mult * rows[n][k : k + 1, :]
    rescale(cols, rows, sub)


def rescale(cols, rows, sub):
    for n, c in enumerate(cols):
        diag = c[0]
        for k in range(1, PANEL):
            diag = jnp.where(sub == k, c[k], diag)
        rows[n] = rows[n] * lax.rsqrt(diag)


def subtract(mat, m, parts, in_diag, order):
    hi, mid, low = [], [], []
    for r in parts:
        h = r.astype(BF16).astype(F32)
        rest = r - h
        c = rest.astype(BF16).astype(F32)
        hi.append(h)
        mid.append(c)
        low.append(rest - c)
    right = jnp.concatenate(hi + mid + hi + low + hi + mid, axis=0).astype(BF16)
    left = jnp.concatenate(hi + hi + mid + hi + low + mid, axis=0).astype(BF16)
    update = lax.dot_general(left, right, (((0,), (0,)), ((), ())), preferred_element_type=F32)
    for t in range(0, order, PANEL):
        mat[m, t : t + PANEL] = (
            jnp.where(in_diag, F32(0.0), mat[m, t : t + PANEL]) - update[t : t + PANEL]
        )


def spread(row, picks):
    return [jnp.take_along_axis(row, pick, axis=1) for pick in picks]


def lower_inverse(mat, xs, blocks, order, first, last):
    lane = lax.broadcasted_iota(jnp.int32, (PANEL, order), 1)
    sub = lax.broadcasted_iota(jnp.int32, (PANEL, order), 0)

    def step(kb, carry):
        r0 = pl.multiple_of(kb * PANEL, PANEL)
        in_diag = (lane >= r0) & (lane < r0 + PANEL)
        unit = jnp.where(lane - r0 == sub, F32(1.0), F32(0.0))
        picks = [jnp.full((PANEL, order), r0 + k, jnp.int32) for k in range(PANEL)]
        rows = [mat[m, pl.ds(r0, PANEL), :] for m in range(blocks)]
        cols = [spread(r, picks) for r in rows]
        rows = [jnp.where(in_diag, unit, r) for r in rows]
        eliminate(cols, rows, sub)
        for m in range(blocks):
            xs[m, pl.ds(r0, PANEL), :] = rows[m]
            subtract(mat, m, [rows[m]], in_diag, order)
        return carry

    lax.fori_loop(first, last, step, 0)


def lower_inverse_wide(mat, xs, blocks, order):
    lane = lax.broadcasted_iota(jnp.int32, (PANEL, order), 1)
    sub = lax.broadcasted_iota(jnp.int32, (PANEL, order), 0)

    def step(kb, carry):
        r0 = pl.multiple_of(kb * 2 * PANEL, 2 * PANEL)
        r1 = pl.multiple_of(r0 + PANEL, PANEL)
        in_top = (lane >= r0) & (lane < r1)
        in_bot = (lane >= r1) & (lane < r1 + PANEL)
        unit_top = jnp.where(lane - r0 == sub, F32(1.0), F32(0.0))
        unit_bot = jnp.where(lane - r1 == sub, F32(1.0), F32(0.0))
        picks = [jnp.full((PANEL, order), r0 + k, jnp.int32) for k in range(2 * PANEL)]
        top = [mat[m, pl.ds(r0, PANEL), :] for m in range(blocks)]
        bot = [mat[m, pl.ds(r1, PANEL), :] for m in range(blocks)]
        ctop = [spread(r, picks[:PANEL]) for r in top]
        cbot = [spread(r, picks[:PANEL]) for r in bot]
        top = [jnp.where(in_top, unit_top, r) for r in top]
        bot = [jnp.where(in_top, F32(0.0), r) for r in bot]
        for k in range(PANEL):
            for n in range(blocks):
                c, b = ctop[n], cbot[n]
                inv = 1.0 / c[k][k : k + 1, :]
                m0 = jnp.where(sub > k, c[k] * inv, F32(0.0))
                m1 = b[k] * inv
                for j in range(k + 1, PANEL):
                    row = c[j][k : k + 1, :]
                    c[j] = c[j] - m0 * row
                    b[j] = b[j] - m1 * row
                row = top[n][k : k + 1, :]
                top[n] = top[n] - m0 * row
                bot[n] = bot[n] - m1 * row
        cols = [spread(r, picks[PANEL:]) for r in bot]
        bot = [jnp.where(in_bot, unit_bot, r) for r in bot]
        rescale(ctop, top, sub)
        eliminate(cols, bot, sub)
        for m in range(blocks):
            upper = jnp.where(in_bot, F32(0.0), top[m])
            xs[m, pl.ds(r0, PANEL), :] = upper
            xs[m, pl.ds(r1, PANEL), :] = bot[m]
            subtract(mat, m, [upper, bot[m]], in_top | in_bot, order)
        return carry

    lax.fori_loop(0, order // (2 * PANEL), step, 0)


def gram_of(x, y, codes, counts, permit, diag, block_at):
    row, lane = iotas(diag.shape[2])
    total = jnp.zeros(row.shape, F32)
    scale = permit[x, pl.ds(y, 1), :]
    for s in range(codes.shape[2]):
        code = codes[x, y, s]
        block = block_at(code // 3, code % 3)
        on = jnp.where(s < counts[x, y], F32(1.0), F32(0.0))
        scaled = ((scale * on) * block.astype(F32)).astype(BF16)
        total = total + lax.dot_general(
            scaled, block, (((1,), (1,)), ((), ())), preferred_element_type=F32
        )
    total = (total + total.T) * F32(0.5)
    return total + jnp.where(row == lane, diag[x, pl.ds(y, 1), :], F32(0.0))


def image_of(factor, vector):
    return lax.dot_general(factor, vector, (((0,), (0,)), ((), ())), preferred_element_type=F32)


def products(x, y, codes, counts, permit, blocks):
    slots = range(codes.shape[2])
    named = [jnp.where(s < counts[x, y], codes[x, y, s], -1) for s in slots]
    scale = permit[x, pl.ds(y, 1), :]
    total = None
    for code, block in blocks:
        times = F32(0.0)
        for c in named:
            times = times + jnp.where(c == code, F32(1.0), F32(0.0))
        scaled = (scale * block.astype(F32)).astype(BF16)
        term = times * lax.dot_general(
            scaled, block, (((1,), (1,)), ((), ())), preferred_element_type=F32
        )
        total = term if total is None else total + term
    return total


def own_gram(codes, counts, permit, own, sums, turned):
    bx, by = own.shape[0], own.shape[1]
    inner = by - 2
    for x in range(bx):
        for y in range(by):
            turned[x * by + y] = own[x, y].T

    def body(g, carry):
        for x in range(bx):
            for u in range(inner // 2):
                y = g * (inner // 2) + u + 1
                blocks = [
                    (3 * (r - x + 1) + dy, turned[r * by + y + dy - 1])
                    for r in range(max(x - 1, 0), min(x + 2, bx))
                    for dy in range(3)
                ]
                sums[x * inner + y - 1] = products(x, y, codes, counts, permit, blocks)
        return carry

    lax.fori_loop(0, 2, body, 0)


def inner_gram(codes, counts, permit, diag, odd, even, sums, mats, xs, turned):
    by = odd.shape[0]
    inner = by - 2
    bx = sums.shape[0] // inner
    order = mats.shape[1]
    px = parity("gx")
    for y in range(by):
        turned[px * by + y] = odd[y].T
        turned[(1 - px) * by + y] = even[y].T
    row, lane = iotas(order)

    def body(g, carry):
        for x in range(bx):
            for u in range(inner // 2):
                y = g * (inner // 2) + u + 1
                blocks = []
                if x == 0:
                    blocks += [(dy, turned[y + dy - 1]) for dy in range(3)]
                if x == bx - 1:
                    blocks += [(6 + dy, turned[by + y + dy - 1]) for dy in range(3)]
                n = x * inner + y - 1
                total = sums[n]
                if blocks:
                    total = total + products(x, y, codes, counts, permit, blocks)
                total = (total + total.T) * F32(0.5)
                mats[n] = total + jnp.where(row == lane, diag[x, pl.ds(y, 1), :], F32(0.0))
        return carry

    lax.fori_loop(0, 2, body, 0)
    lower_inverse(mats, xs, bx * inner, order, 0, EARLY)


def edge_all(
    codes, counts, weights, permit, diag, own_turned, far_turned, odd, even, vectors,
    factors, acc, to_odd, to_even, turned, mats, xs,
):
    bx, by = vectors.shape[0], vectors.shape[1]
    order = mats.shape[1]
    px, py = parity("gx"), parity("gy")
    for p in range(bx + 2):
        row = px * (bx + 1) if p == 0 else (1 - px) * (bx + 1) if p == bx + 1 else p
        turned[row * 6 + 5 * py] = odd[p].T
        turned[row * 6 + 5 * (1 - py)] = even[p].T
        for n, y in enumerate((0, 1, by - 2, by - 1)):
            if 0 < p < bx + 1:
                turned[p * 6 + 1 + n] = own_turned[(p - 1) * by + y]
            else:
                turned[p * 6 + 1 + n] = far_turned[p // (bx + 1) * by + y]
    edges = [(x, side) for x in range(bx) for side in range(2)]
    for m, (x, side) in enumerate(edges):
        mats[m] = gram_of(
            x, side * (by - 1), codes, counts, permit, diag,
            lambda dx, dy: turned[(x + dx) * 6 + side * 3 + dy],
        )
    lower_inverse_wide(mats, xs, len(edges), order)
    acc[...] = jnp.zeros(acc.shape, acc.dtype)
    row, lane = iotas(order)
    images = []
    for m, (x, side) in enumerate(edges):
        f = jnp.where(lane <= row, xs[m], F32(0.0)).astype(BF16)
        factors[m] = f
        images.append(image_of(f, vectors[x, side * (by - 1)]))
    for m, (x, side) in enumerate(edges):
        y = side * (by - 1)

        def add(s, c):
            code = codes[x, y, s]
            n = (x + code // 3) * 6 + side * 3 + code % 3
            acc[n] = acc[n] + weights[x, y, s] * images[m]
            return c

        lax.fori_loop(0, counts[x, y], add, 0)
    for p in range(bx + 2):
        to_odd[p] = acc[p * 6 + 5 * py].astype(BF16)
        to_even[p] = acc[p * 6 + 5 * (1 - py)].astype(BF16)


def inner_all(
    codes, counts, weights, mats_in, xs_in, edge_acc, edge_factors, vectors,
    factor, acc, mats, xs,
):
    bx, by = vectors.shape[0], vectors.shape[1]
    inner = by - 2
    order = mats.shape[1]
    done = EARLY * PANEL
    mats[:, done:] = mats_in[:, done:]
    xs[:, :done] = xs_in[:, :done]
    lower_inverse(mats, xs, bx * inner, order, EARLY, order // PANEL)
    zero = jnp.zeros(acc.shape[1:], F32)
    for p in range(bx + 2):
        for y in range(2, by - 2):
            acc[p * by + y] = zero
        for n, y in enumerate((0, 1, by - 2, by - 1)):
            acc[p * by + y] = edge_acc[p * 6 + 1 + n]
    for x in range(bx):
        factor[x, 0] = edge_factors[2 * x]
        factor[x, by - 1] = edge_factors[2 * x + 1]
    row, lane = iotas(order)

    def body(h, carry):
        x = h // (inner // 2)
        images = []
        for u in range(2):
            y = (h % (inner // 2)) * 2 + u + 1
            f = jnp.where(lane <= row, xs[x * inner + y - 1], F32(0.0)).astype(BF16)
            factor[x, y] = f
            images.append(image_of(f, vectors[x, y]))
        for u in range(2):
            y = (h % (inner // 2)) * 2 + u + 1

            def add(s, c):
                code = codes[x, y, s]
                n = (x + code // 3) * by + y + code % 3 - 1
                acc[n] = acc[n] + weights[x, y, s] * images[u]
                return c

            lax.fori_loop(0, counts[x, y], add, 0)
        return carry

    lax.fori_loop(0, bx * inner // 2, body, 0)


def close_halo(acc, odd, even, to_odd, to_even):
    by = to_odd.shape[0]
    last = odd.shape[0] - 1
    px, py = parity("gx"), parity("gy")
    for out, h in ((to_odd, px), (to_even, 1 - px)):
        row = h * last * by
        for y in range(1, by - 1):
            out[y] = acc[row + y].astype(BF16)
        for terms, y in ((odd, (by - 1) * py), (even, (by - 1) * (1 - py))):
            out[y] = (acc[row + y] + terms[h * last].astype(F32)).astype(BF16)


def collect(acc, odd_x, even_x, odd_y, even_y, out):
    bx, by = out.shape[0], out.shape[1]
    px, py = parity("gx"), parity("gy")
    for terms, x in ((odd_x, (bx - 1) * px), (even_x, (bx - 1) * (1 - px))):
        row = (x + 1) * by
        for y in range(1, by - 1):
            out[x, y] = (acc[row + y] + terms[y].astype(F32)).astype(BF16)
        for more, y in ((odd_y, (by - 1) * py), (even_y, (by - 1) * (1 - py))):
            v = acc[row + y] + terms[y].astype(F32) + more[x + 1].astype(F32)
            out[x, y] = v.astype(BF16)


def local(coeffs, permit, diag, codes, counts, weights, vectors):
    bx, by, coupling, order = coeffs.shape
    width = vectors.shape[3]
    rows, inner = bx + 2, by - 2
    shape = jax.ShapeDtypeStruct
    px, py = parity("gx"), parity("gy")
    pick = lax.dynamic_index_in_dim

    def column(y):
        return jnp.concatenate([pick(odd_x, y, 0), pick(coeffs, y, 1, False), pick(even_x, y, 0)])

    again = lax.optimization_barrier(coeffs)
    even_x = swap(pick(again, (bx - 1) * (1 - px), 0, False), "gx", 0)
    odd_x = swap(pick(coeffs, (bx - 1) * px, 0, False), "gx", 1)
    odd_y = swap(column((by - 1) * py), "gy", 1)
    even_y = swap(column((by - 1) * (1 - py)), "gy", 0)
    sums, own_turned = call(
        own_gram,
        (shape((bx * inner, order, order), F32), shape((bx * by, order, coupling), BF16)),
        [SMEM] * 2 + [VMEM] * 2, [], "own_gram", 12, 4 * 10**9,
    )(codes, counts, permit, coeffs)
    mats, xs, far_turned = call(
        inner_gram,
        (
            shape((bx * inner, order, order), F32),
            shape((bx * inner, order, order), F32),
            shape((2 * by, order, coupling), BF16),
        ),
        [SMEM] * 2 + [VMEM] * 5, [], "inner_gram", 16, 6 * 10**9,
    )(codes, counts, permit, diag, odd_x, even_x, sums)
    edge_factors, edge_acc, to_odd, to_even = call(
        edge_all,
        (
            shape((2 * bx, order, order), BF16),
            shape((rows * 6, order, width), F32),
            shape((rows, order, width), BF16),
            shape((rows, order, width), BF16),
        ),
        [SMEM] * 3 + [VMEM] * 7,
        [
            pltpu.VMEM((rows * 6, order, coupling), BF16),
            pltpu.VMEM((2 * bx, order, order), F32),
            pltpu.VMEM((2 * bx, order, order), F32),
        ],
        "edge_all", 16, 8 * 10**9,
    )(codes, counts, weights, permit, diag, own_turned, far_turned, odd_y, even_y, vectors)
    from_odd_y = swap(to_odd, "gy", 1)
    from_even_y = swap(to_even, "gy", 0)
    factor, acc = call(
        inner_all,
        (
            shape((bx, by, order, order), BF16),
            shape((rows * by, order, width), F32),
        ),
        [SMEM] * 3 + [VMEM] * 5,
        [
            pltpu.VMEM((bx * inner, order, order), F32),
            pltpu.VMEM((bx * inner, order, order), F32),
        ],
        "inner_all", 20, 12 * 10**9,
    )(codes, counts, weights, mats, xs, edge_acc, edge_factors, vectors)
    to_odd, to_even = call(
        close_halo,
        (shape((by, order, width), BF16), shape((by, order, width), BF16)),
        [VMEM] * 3, [], "close_halo", 8, 10**8,
    )(acc, from_odd_y, from_even_y)
    from_odd_x = swap(to_odd, "gx", 1)
    from_even_x = swap(to_even, "gx", 0)
    applied = call(
        collect, shape((bx, by, order, width), BF16), [VMEM] * 5, [], "collect", 8, 10**8,
    )(acc, from_odd_x, from_even_x, from_odd_y, from_even_y)
    return factor, applied


def solution(mesh):
    placed = (
        P("gx", "gy", None, None),
        P("gx", "gy", None),
        P("gx", "gy", None),
        P("gx", "gy", None),
        P("gx", "gy"),
        P("gx", "gy", None),
        P("gx", "gy", None, None),
    )
    return jax.shard_map(
        local,
        mesh=mesh,
        in_specs=placed,
        out_specs=(P("gx", "gy", None, None), P("gx", "gy", None, None)),
        check_vma=False,
    )
```

```python
import jax
import jax.numpy as jnp
from jax import lax
from jax.experimental import pallas as pl
from jax.experimental.pallas import tpu as pltpu
from jax.sharding import PartitionSpec as P

PANEL = 8
EARLY = 8
BF16, F32 = jnp.bfloat16, jnp.float32
VMEM = pl.BlockSpec(memory_space=pltpu.VMEM)
SMEM = pl.BlockSpec(memory_space=pltpu.SMEM)


def call(body, outs, ins, scratch, name, mib, flops):
    return pl.pallas_call(
        body,
        out_shape=outs,
        in_specs=ins,
        out_specs=jax.tree.map(lambda _: VMEM, outs),
        scratch_shapes=scratch,
        compiler_params=pltpu.CompilerParams(vmem_limit_bytes=mib * 1024 * 1024),
        cost_estimate=pl.CostEstimate(flops=flops, bytes_accessed=4 * 1024 * 1024, transcendentals=0),
        name=name,
    )


def swap(value, axis, first):
    pairs = []
    for i in range(first, lax.axis_size(axis) - 1, 2):
        pairs += [(i, i + 1), (i + 1, i)]
    return lax.ppermute(value, axis, pairs)


def parity(axis):
    return lax.rem(lax.axis_index(axis), 2)


def iotas(order):
    return (
        lax.broadcasted_iota(jnp.int32, (order, order), 0),
        lax.broadcasted_iota(jnp.int32, (order, order), 1),
    )


def eliminate(cols, rows, sub):
    for k in range(PANEL):
        for n, c in enumerate(cols):
            inv = 1.0 / c[k][k : k + 1, :]
            mult = jnp.where(sub > k, c[k] * inv, F32(0.0))
            for j in range(k + 1, PANEL):
                c[j] = c[j] - mult * c[j][k : k + 1, :]
            rows[n] = rows[n] - mult * rows[n][k : k + 1, :]
    rescale(cols, rows, sub)


def rescale(cols, rows, sub):
    for n, c in enumerate(cols):
        diag = c[0]
        for k in range(1, PANEL):
            diag = jnp.where(sub == k, c[k], diag)
        rows[n] = rows[n] * lax.rsqrt(diag)


def subtract(mat, m, parts, in_diag, order):
    hi, mid, low = [], [], []
    for r in parts:
        h = r.astype(BF16).astype(F32)
        rest = r - h
        c = rest.astype(BF16).astype(F32)
        hi.append(h)
        mid.append(c)
        low.append(rest - c)
    right = jnp.concatenate(hi + mid + hi + low + hi + mid, axis=0).astype(BF16)
    left = jnp.concatenate(hi + hi + mid + hi + low + mid, axis=0).astype(BF16)
    update = lax.dot_general(left, right, (((0,), (0,)), ((), ())), preferred_element_type=F32)
    for t in range(0, order, PANEL):
        mat[m, t : t + PANEL] = (
            jnp.where(in_diag, F32(0.0), mat[m, t : t + PANEL]) - update[t : t + PANEL]
        )


def spread(row, picks):
    return [jnp.take_along_axis(row, pick, axis=1) for pick in picks]


def lower_inverse(mat, xs, blocks, order, first, last):
    lane = lax.broadcasted_iota(jnp.int32, (PANEL, order), 1)
    sub = lax.broadcasted_iota(jnp.int32, (PANEL, order), 0)

    def step(kb, carry):
        r0 = pl.multiple_of(kb * PANEL, PANEL)
        in_diag = (lane >= r0) & (lane < r0 + PANEL)
        unit = jnp.where(lane - r0 == sub, F32(1.0), F32(0.0))
        picks = [jnp.full((PANEL, order), r0 + k, jnp.int32) for k in range(PANEL)]
        rows = [mat[m, pl.ds(r0, PANEL), :] for m in range(blocks)]
        cols = [spread(r, picks) for r in rows]
        rows = [jnp.where(in_diag, unit, r) for r in rows]
        eliminate(cols, rows, sub)
        for m in range(blocks):
            xs[m, pl.ds(r0, PANEL), :] = rows[m]
            subtract(mat, m, [rows[m]], in_diag, order)
        return carry

    lax.fori_loop(first, last, step, 0)


def lower_inverse_wide(mat, xs, blocks, order):
    lane = lax.broadcasted_iota(jnp.int32, (PANEL, order), 1)
    sub = lax.broadcasted_iota(jnp.int32, (PANEL, order), 0)

    def step(kb, carry):
        r0 = pl.multiple_of(kb * 2 * PANEL, 2 * PANEL)
        r1 = pl.multiple_of(r0 + PANEL, PANEL)
        in_top = (lane >= r0) & (lane < r1)
        in_bot = (lane >= r1) & (lane < r1 + PANEL)
        unit_top = jnp.where(lane - r0 == sub, F32(1.0), F32(0.0))
        unit_bot = jnp.where(lane - r1 == sub, F32(1.0), F32(0.0))
        picks = [jnp.full((PANEL, order), r0 + k, jnp.int32) for k in range(2 * PANEL)]
        top = [mat[m, pl.ds(r0, PANEL), :] for m in range(blocks)]
        bot = [mat[m, pl.ds(r1, PANEL), :] for m in range(blocks)]
        ctop = [spread(r, picks[:PANEL]) for r in top]
        cbot = [spread(r, picks[:PANEL]) for r in bot]
        top = [jnp.where(in_top, unit_top, r) for r in top]
        bot = [jnp.where(in_top, F32(0.0), r) for r in bot]
        for k in range(PANEL):
            for n in range(blocks):
                c, b = ctop[n], cbot[n]
                inv = 1.0 / c[k][k : k + 1, :]
                m0 = jnp.where(sub > k, c[k] * inv, F32(0.0))
                m1 = b[k] * inv
                for j in range(k + 1, PANEL):
                    row = c[j][k : k + 1, :]
                    c[j] = c[j] - m0 * row
                    b[j] = b[j] - m1 * row
                row = top[n][k : k + 1, :]
                top[n] = top[n] - m0 * row
                bot[n] = bot[n] - m1 * row
        cols = [spread(r, picks[PANEL:]) for r in bot]
        bot = [jnp.where(in_bot, unit_bot, r) for r in bot]
        rescale(ctop, top, sub)
        eliminate(cols, bot, sub)
        for m in range(blocks):
            upper = jnp.where(in_bot, F32(0.0), top[m])
            xs[m, pl.ds(r0, PANEL), :] = upper
            xs[m, pl.ds(r1, PANEL), :] = bot[m]
            subtract(mat, m, [upper, bot[m]], in_top | in_bot, order)
        return carry

    lax.fori_loop(0, order // (2 * PANEL), step, 0)


def gram_of(x, y, codes, counts, permit, diag, block_at):
    row, lane = iotas(diag.shape[2])
    total = jnp.zeros(row.shape, F32)
    scale = permit[x, pl.ds(y, 1), :]
    for s in range(codes.shape[2]):
        code = codes[x, y, s]
        block = block_at(code // 3, code % 3)
        on = jnp.where(s < counts[x, y], F32(1.0), F32(0.0))
        scaled = ((scale * on) * block.astype(F32)).astype(BF16)
        total = total + lax.dot_general(
            scaled, block, (((1,), (1,)), ((), ())), preferred_element_type=F32
        )
    total = (total + total.T) * F32(0.5)
    return total + jnp.where(row == lane, diag[x, pl.ds(y, 1), :], F32(0.0))


def image_of(factor, vector):
    return lax.dot_general(factor, vector, (((0,), (0,)), ((), ())), preferred_element_type=F32)


def products(x, y, codes, counts, permit, blocks):
    slots = range(codes.shape[2])
    named = [jnp.where(s < counts[x, y], codes[x, y, s], -1) for s in slots]
    scale = permit[x, pl.ds(y, 1), :]
    total = None
    for code, block in blocks:
        times = F32(0.0)
        for c in named:
            times = times + jnp.where(c == code, F32(1.0), F32(0.0))
        scaled = (scale * block.astype(F32)).astype(BF16)
        term = times * lax.dot_general(
            scaled, block, (((1,), (1,)), ((), ())), preferred_element_type=F32
        )
        total = term if total is None else total + term
    return total


def own_gram(codes, counts, permit, own, sums, turned):
    bx, by = own.shape[0], own.shape[1]
    inner = by - 2
    for x in range(bx):
        for y in range(by):
            turned[x * by + y] = own[x, y].T

    def body(g, carry):
        for x in range(bx):
            for u in range(inner // 2):
                y = g * (inner // 2) + u + 1
                blocks = [
                    (3 * (r - x + 1) + dy, turned[r * by + y + dy - 1])
                    for r in range(max(x - 1, 0), min(x + 2, bx))
                    for dy in range(3)
                ]
                sums[x * inner + y - 1] = products(x, y, codes, counts, permit, blocks)
        return carry

    lax.fori_loop(0, 2, body, 0)


def inner_gram(codes, counts, permit, diag, odd, even, sums, mats, xs, turned):
    by = odd.shape[0]
    inner = by - 2
    bx = sums.shape[0] // inner
    order = mats.shape[1]
    px = parity("gx")
    for y in range(by):
        turned[px * by + y] = odd[y].T
        turned[(1 - px) * by + y] = even[y].T
    row, lane = iotas(order)

    def body(g, carry):
        for x in range(bx):
            for u in range(inner // 2):
                y = g * (inner // 2) + u + 1
                blocks = []
                if x == 0:
                    blocks += [(dy, turned[y + dy - 1]) for dy in range(3)]
                if x == bx - 1:
                    blocks += [(6 + dy, turned[by + y + dy - 1]) for dy in range(3)]
                n = x * inner + y - 1
                total = sums[n]
                if blocks:
                    total = total + products(x, y, codes, counts, permit, blocks)
                total = (total + total.T) * F32(0.5)
                mats[n] = total + jnp.where(row == lane, diag[x, pl.ds(y, 1), :], F32(0.0))
        return carry

    lax.fori_loop(0, 2, body, 0)
    lower_inverse(mats, xs, bx * inner, order, 0, EARLY)


def edge_all(
    codes, counts, weights, permit, diag, own_turned, far_turned, odd, even, vectors,
    factors, acc, to_odd, to_even, turned, mats, xs,
):
    bx, by = vectors.shape[0], vectors.shape[1]
    order = mats.shape[1]
    px, py = parity("gx"), parity("gy")
    for p in range(bx + 2):
        row = px * (bx + 1) if p == 0 else (1 - px) * (bx + 1) if p == bx + 1 else p
        turned[row * 6 + 5 * py] = odd[p].T
        turned[row * 6 + 5 * (1 - py)] = even[p].T
        for n, y in enumerate((0, 1, by - 2, by - 1)):
            if 0 < p < bx + 1:
                turned[p * 6 + 1 + n] = own_turned[(p - 1) * by + y]
            else:
                turned[p * 6 + 1 + n] = far_turned[p // (bx + 1) * by + y]
    edges = [(x, side) for x in range(bx) for side in range(2)]
    for m, (x, side) in enumerate(edges):
        mats[m] = gram_of(
            x, side * (by - 1), codes, counts, permit, diag,
            lambda dx, dy: turned[(x + dx) * 6 + side * 3 + dy],
        )
    lower_inverse_wide(mats, xs, len(edges), order)
    acc[...] = jnp.zeros(acc.shape, acc.dtype)
    row, lane = iotas(order)
    images = []
    for m, (x, side) in enumerate(edges):
        f = jnp.where(lane <= row, xs[m], F32(0.0)).astype(BF16)
        factors[m] = f
        images.append(image_of(f, vectors[x, side * (by - 1)]))
    for m, (x, side) in enumerate(edges):
        y = side * (by - 1)

        def add(s, c):
            code = codes[x, y, s]
            n = (x + code // 3) * 6 + side * 3 + code % 3
            acc[n] = acc[n] + weights[x, y, s] * images[m]
            return c

        lax.fori_loop(0, counts[x, y], add, 0)
    for p in range(bx + 2):
        to_odd[p] = acc[p * 6 + 5 * py].astype(BF16)
        to_even[p] = acc[p * 6 + 5 * (1 - py)].astype(BF16)


def inner_all(
    codes, counts, weights, mats_in, xs_in, edge_acc, edge_factors, vectors,
    factor, acc, mats, xs,
):
    bx, by = vectors.shape[0], vectors.shape[1]
    inner = by - 2
    order = mats.shape[1]
    done = EARLY * PANEL
    mats[:, done:] = mats_in[:, done:]
    xs[:, :done] = xs_in[:, :done]
    lower_inverse(mats, xs, bx * inner, order, EARLY, order // PANEL)
    zero = jnp.zeros(acc.shape[1:], F32)
    for p in range(bx + 2):
        for y in range(2, by - 2):
            acc[p * by + y] = zero
        for n, y in enumerate((0, 1, by - 2, by - 1)):
            acc[p * by + y] = edge_acc[p * 6 + 1 + n]
    for x in range(bx):
        factor[x, 0] = edge_factors[2 * x]
        factor[x, by - 1] = edge_factors[2 * x + 1]
    row, lane = iotas(order)

    def body(x, carry):
        images = []
        for u in range(inner):
            y = u + 1
            f = jnp.where(lane <= row, xs[x * inner + y - 1], F32(0.0)).astype(BF16)
            factor[x, y] = f
            images.append(image_of(f, vectors[x, y]))
        for u in range(inner):
            y = u + 1

            def add(s, c):
                code = codes[x, y, s]
                n = (x + code // 3) * by + y + code % 3 - 1
                acc[n] = acc[n] + weights[x, y, s] * images[u]
                return c

            lax.fori_loop(0, counts[x, y], add, 0)
        return carry

    lax.fori_loop(0, bx, body, 0)


def close_halo(acc, odd, even, to_odd, to_even):
    by = to_odd.shape[0]
    last = odd.shape[0] - 1
    px, py = parity("gx"), parity("gy")
    for out, h in ((to_odd, px), (to_even, 1 - px)):
        row = h * last * by
        for y in range(1, by - 1):
            out[y] = acc[row + y].astype(BF16)
        for terms, y in ((odd, (by - 1) * py), (even, (by - 1) * (1 - py))):
            out[y] = (acc[row + y] + terms[h * last].astype(F32)).astype(BF16)


def collect(acc, odd_x, even_x, odd_y, even_y, out):
    bx, by = out.shape[0], out.shape[1]
    px, py = parity("gx"), parity("gy")
    for terms, x in ((odd_x, (bx - 1) * px), (even_x, (bx - 1) * (1 - px))):
        row = (x + 1) * by
        for y in range(1, by - 1):
            out[x, y] = (acc[row + y] + terms[y].astype(F32)).astype(BF16)
        for more, y in ((odd_y, (by - 1) * py), (even_y, (by - 1) * (1 - py))):
            v = acc[row + y] + terms[y].astype(F32) + more[x + 1].astype(F32)
            out[x, y] = v.astype(BF16)


def local(coeffs, permit, diag, codes, counts, weights, vectors):
    bx, by, coupling, order = coeffs.shape
    width = vectors.shape[3]
    rows, inner = bx + 2, by - 2
    shape = jax.ShapeDtypeStruct
    px, py = parity("gx"), parity("gy")
    pick = lax.dynamic_index_in_dim

    def column(y):
        return jnp.concatenate([pick(odd_x, y, 0), pick(coeffs, y, 1, False), pick(even_x, y, 0)])

    again = lax.optimization_barrier(coeffs)
    even_x = swap(pick(again, (bx - 1) * (1 - px), 0, False), "gx", 0)
    odd_x = swap(pick(coeffs, (bx - 1) * px, 0, False), "gx", 1)
    odd_y = swap(column((by - 1) * py), "gy", 1)
    even_y = swap(column((by - 1) * (1 - py)), "gy", 0)
    sums, own_turned = call(
        own_gram,
        (shape((bx * inner, order, order), F32), shape((bx * by, order, coupling), BF16)),
        [SMEM] * 2 + [VMEM] * 2, [], "own_gram", 12, 4 * 10**9,
    )(codes, counts, permit, coeffs)
    mats, xs, far_turned = call(
        inner_gram,
        (
            shape((bx * inner, order, order), F32),
            shape((bx * inner, order, order), F32),
            shape((2 * by, order, coupling), BF16),
        ),
        [SMEM] * 2 + [VMEM] * 5, [], "inner_gram", 16, 6 * 10**9,
    )(codes, counts, permit, diag, odd_x, even_x, sums)
    edge_factors, edge_acc, to_odd, to_even = call(
        edge_all,
        (
            shape((2 * bx, order, order), BF16),
            shape((rows * 6, order, width), F32),
            shape((rows, order, width), BF16),
            shape((rows, order, width), BF16),
        ),
        [SMEM] * 3 + [VMEM] * 7,
        [
            pltpu.VMEM((rows * 6, order, coupling), BF16),
            pltpu.VMEM((2 * bx, order, order), F32),
            pltpu.VMEM((2 * bx, order, order), F32),
        ],
        "edge_all", 16, 8 * 10**9,
    )(codes, counts, weights, permit, diag, own_turned, far_turned, odd_y, even_y, vectors)
    from_odd_y = swap(to_odd, "gy", 1)
    from_even_y = swap(to_even, "gy", 0)
    factor, acc = call(
        inner_all,
        (
            shape((bx, by, order, order), BF16),
            shape((rows * by, order, width), F32),
        ),
        [SMEM] * 3 + [VMEM] * 5,
        [
            pltpu.VMEM((bx * inner, order, order), F32),
            pltpu.VMEM((bx * inner, order, order), F32),
        ],
        "inner_all", 20, 12 * 10**9,
    )(codes, counts, weights, mats, xs, edge_acc, edge_factors, vectors)
    to_odd, to_even = call(
        close_halo,
        (shape((by, order, width), BF16), shape((by, order, width), BF16)),
        [VMEM] * 3, [], "close_halo", 8, 10**8,
    )(acc, from_odd_y, from_even_y)
    from_odd_x = swap(to_odd, "gx", 1)
    from_even_x = swap(to_even, "gx", 0)
    applied = call(
        collect, shape((bx, by, order, width), BF16), [VMEM] * 5, [], "collect", 8, 10**8,
    )(acc, from_odd_x, from_even_x, from_odd_y, from_even_y)
    return factor, applied


def solution(mesh):
    placed = (
        P("gx", "gy", None, None),
        P("gx", "gy", None),
        P("gx", "gy", None),
        P("gx", "gy", None),
        P("gx", "gy"),
        P("gx", "gy", None),
        P("gx", "gy", None, None),
    )
    return jax.shard_map(
        local,
        mesh=mesh,
        in_specs=placed,
        out_specs=(P("gx", "gy", None, None), P("gx", "gy", None, None)),
        check_vma=False,
    )
```
